32 devices in a mesh: bins: 8 (over y, x, core), batch: 4 (over z).
Axes of the slice: x: 2, y: 2, z: 4, core: 2. Of those that a mesh axis runs over, the one named last changes fastest.
Arguments:
- block_in: bfloat16 [16, 2048, 768], P('batch', 'bins')
- gain_in: float32 [768], replicated, may hold values from 0.5 to 1.5
- shift_in: float32 [768], replicated, may hold values from -2 to 2
- dilated_taps_weight: bfloat16 [3, 768, 384], replicated, may hold values from -0.125 to 0.125
- gain_mid: float32 [384], replicated, may hold values from 0.5 to 1.5
- shift_mid: float32 [384], replicated, may hold values from -2 to 2
- proj_weight: bfloat16 [384, 768], replicated, may hold values from -0.3125 to 0.3125
- proj_bias: float32 [768], replicated, may hold values from -2 to 2
- head_human: bfloat16 [768, 5313], replicated, may hold values from -0.21875 to 0.21875
- bias_human: float32 [5313], replicated, may hold values from -3 to 3
- head_mouse: bfloat16 [768, 1643], replicated, may hold values from -0.21875 to 0.21875
- bias_mouse: float32 [1643], replicated, may hold values from -3 to 3
- species: int32 [16], P('batch'), may hold values 0 or 1
- counts: int32 [16, 2048, 5313], P('batch', 'bins'), may hold values from 0 to 5
Outputs:
- block_out: bfloat16 [16, 2048, 768], P('batch', 'bins')
- input_grad: bfloat16 [16, 2048, 768], P('batch', 'bins')
- gain_in_grad: float32 [768], replicated
- shift_in_grad: float32 [768], replicated
- conv_grad: float32 [3, 768, 384], replicated
- gain_mid_grad: float32 [384], replicated
- shift_mid_grad: float32 [384], replicated
- proj_grad: float32 [384, 768], replicated
- proj_bias_grad: float32 [768], replicated
- head_human_grad: float32 [768, 5313], replicated
- bias_human_grad: float32 [5313], replicated
- head_mouse_grad: float32 [768, 1643], replicated
- bias_mouse_grad: float32 [1643], replicated
The draws below stay inside these ranges and needn't reach their ends.
Inputs may be any that keep to these rules, and one draw needn't show every extreme that they name: `species`: 0 marks a human window, 1 a mouse window.
All inputs are finite; a program needn't handle non-finite values. No bound on the sum of `species` on one device may be relied on, other than what follows from the above.
Results may differ from the reference program's by a relative error of at most 0.0063.
Values may be sent and summed in bfloat16 or wider, within the bound.
No kernel may reach another device: no remote copies, remote signals or barrier semaphores. Data moves between devices by JAX's collectives and lax.ppermute only.
A program may use at most 192 MiB of HBM per device.

```python
import math
import jax
import jax.numpy as jnp
from jax import lax

D = 768
F = 384
TH = 5313
TM = 1643
DILATION_STEP = 11
WINDOW_BINS = 2048
WINDOWS = 16


def draw_block_in(key, part):
    noise_key, centre_key = jax.random.split(key, 2)
    position = jnp.arange(WINDOW_BINS, dtype=jnp.float32) / WINDOW_BINS
    window_rank = jnp.arange(WINDOWS, dtype=jnp.float32) / WINDOWS
    scaling = 0.6 * jnp.exp(jnp.log(3.0) * position)[None, :, None] * (0.8 + 0.6 * window_rank)[:, None, None]
    centre = 0.5 * jax.random.normal(centre_key, (D,), jnp.float32)
    noise = jax.random.normal(noise_key, (WINDOWS, WINDOW_BINS, D), jnp.float32)
    return ((centre + noise) * scaling).astype(jnp.bfloat16)


def place_ends(result, stream_key, low, high):
    longest = result.shape.index(max(result.shape))
    spots = []
    for shift in (0, 1):
        where = [jax.random.randint(jax.random.fold_in(stream_key, axis), (), 0, length) for axis, length in enumerate(result.shape)]
        where[longest] = (where[longest] + shift) % result.shape[longest]
        spots.append(tuple(where))
    return result.at[spots[0]].set(low).at[spots[1]].set(high)


def centred(stream_key, dims, scale, limit, held_as=jnp.bfloat16):
    return jnp.clip(scale * jax.random.normal(stream_key, dims, jnp.float32), -limit, limit).astype(held_as)


def setup_inputs(seed: int = 0) -> dict:
    keys = jax.random.split(jax.random.key(seed), 15)
    return {
        "block_in": draw_block_in(jax.random.fold_in(keys[14], 71), 0),
        "gain_in": jnp.clip(1.0 + 0.1 * jax.random.normal(keys[1], (D,), jnp.float32), 0.5, 1.5),
        "shift_in": centred(keys[2], (D,), 0.3, 2.0, jnp.float32),
        "dilated_taps_weight": centred(keys[3], (3, D, F), (3 * D) ** -0.5, 0.125),
        "gain_mid": jnp.clip(1.0 + 0.1 * jax.random.normal(keys[4], (F,), jnp.float32), 0.5, 1.5),
        "shift_mid": centred(keys[5], (F,), 0.3, 2.0, jnp.float32),
        "proj_weight": centred(keys[6], (F, D), F ** -0.5, 0.3125),
        "proj_bias": centred(keys[7], (D,), 0.3, 2.0, jnp.float32),
        "head_human": centred(keys[8], (D, TH), D ** -0.5, 0.21875),
        "bias_human": centred(keys[9], (TH,), 0.5, 3.0, jnp.float32),
        "head_mouse": centred(keys[10], (D, TM), D ** -0.5, 0.21875),
        "bias_mouse": centred(keys[11], (TM,), 0.5, 3.0, jnp.float32),
        "species": place_ends((jax.random.randint(keys[12], (WINDOWS,), 0, 4) < 1).astype(jnp.int32), jax.random.fold_in(keys[12], 1), 0, 1),
        "counts": place_ends(jax.random.randint(keys[13], (WINDOWS, WINDOW_BINS, TH), 0, 6), jax.random.fold_in(keys[13], 1), 0, 5).astype(jnp.int32),
    }


EPS = 1e-05
TOP_PRECISION = lax.Precision.HIGHEST

@jax.custom_vjp
def low(v):
    return lax.optimization_barrier(v.astype(jnp.bfloat16)).astype(jnp.float32)

@jax.custom_vjp
def low_back(v):
    return v

def low_keep(v):
    return (low(v), None)

def low_pass(kept, grad):
    return (grad,)

def back_keep(v):
    return (v, None)

def back_low(kept, grad):
    return (low(grad),)
low.defvjp(low_keep, low_pass)
low_back.defvjp(back_keep, back_low)

def activate(values):
    return values * jax.nn.sigmoid(1.702 * values)

def batch_norm(values, gain, shift):
    flat = values.reshape(-1, values.shape[-1])
    population = flat.shape[0]
    centre = lax.optimization_barrier(jnp.sum(flat, axis=0)) / population
    spread = lax.optimization_barrier(jnp.sum(flat * flat, axis=0)) / population - centre * centre
    return (values - centre) * lax.rsqrt(spread + EPS) * gain + shift

def head_loss(outputs, mouse_rows, counted, head_human, bias_human, head_mouse, bias_mouse):
    logits_human = low_back(jnp.dot(outputs, head_human, precision=TOP_PRECISION)) + bias_human
    logits_mouse = low_back(jnp.dot(outputs, head_mouse, precision=TOP_PRECISION)) + bias_mouse
    rate_human = jax.nn.softplus(logits_human)
    rate_mouse = jax.nn.softplus(logits_mouse)
    loss_human = lax.optimization_barrier(jnp.sum(rate_human - counted * jnp.log(rate_human), axis=1)) * math.sqrt(D / TH)
    loss_mouse = lax.optimization_barrier(jnp.sum(rate_mouse - counted[:, :TM] * jnp.log(rate_mouse), axis=1)) * math.sqrt(D / TM)
    return jnp.sum((1.0 - mouse_rows) * loss_human + mouse_rows * loss_mouse)

def forward(block_in, gain_in, shift_in, dilated_taps_weight, gain_mid, shift_mid, proj_weight, proj_bias, head_human, bias_human, head_mouse, bias_mouse, mouse, counted):
    hidden_input = low(activate(batch_norm(block_in, gain_in, shift_in)))
    padded_rows = jnp.pad(hidden_input, ((0, 0), (DILATION_STEP, DILATION_STEP), (0, 0)))
    dilated_output = jnp.zeros((WINDOWS, WINDOW_BINS, F), jnp.float32)
    for tap_shift in range(3):
        dilated_output = dilated_output + jnp.einsum('cgi,iy->cgy', padded_rows[:, tap_shift * DILATION_STEP:tap_shift * DILATION_STEP + WINDOW_BINS], dilated_taps_weight[tap_shift], precision=TOP_PRECISION)
    dilated_output = low_back(dilated_output)
    hidden_mid = low(activate(batch_norm(dilated_output, gain_mid, shift_mid)))
    branch = low_back(jnp.einsum('wtf,fd->wtd', hidden_mid, proj_weight, precision=TOP_PRECISION))
    outputs = low(block_in + branch + proj_bias)
    grouped_mouse = jnp.repeat(mouse, WINDOW_BINS).reshape(WINDOWS, WINDOW_BINS)
    checked = jax.checkpoint(head_loss)

    def one_group(group):
        return checked(group[0], group[1], group[2], head_human, bias_human, head_mouse, bias_mouse)
    losses = lax.map(one_group, (outputs, grouped_mouse, counted))
    return (jnp.sum(losses), outputs)

def reference(block_in, gain_in, shift_in, dilated_taps_weight, gain_mid, shift_mid, proj_weight, proj_bias, head_human, bias_human, head_mouse, bias_mouse, species, counts):
    mouse = species.astype(jnp.float32)
    counted = counts.astype(jnp.float32)
    primals = (block_in.astype(jnp.float32), gain_in, shift_in, dilated_taps_weight.astype(jnp.float32), gain_mid, shift_mid, proj_weight.astype(jnp.float32), proj_bias, head_human.astype(jnp.float32), bias_human, head_mouse.astype(jnp.float32), bias_mouse)

    def loss_only(*params):
        return forward(*params, mouse, counted)
    loss, pull, outputs = jax.vjp(loss_only, *primals, has_aux=True)
    grads = pull(jnp.ones_like(loss))
    return (outputs.astype(jnp.bfloat16), grads[0].astype(jnp.bfloat16), grads[1], grads[2], grads[3], grads[4], grads[5], grads[6], grads[7], grads[8], grads[9], grads[10], grads[11])
```

```python
import functools
import math

import jax
import jax.numpy as jnp
from jax import lax
from jax.experimental import pallas as pl
from jax.experimental.pallas import tpu as pltpu
from jax.sharding import PartitionSpec as P

DILATION_STEP = 11
EPS = 1e-05
F32 = jnp.float32
BF16 = jnp.bfloat16
EVERY = ("bins", "batch")
LANES = 128
TILE = 768


def bits_of(size):
    return [1 << i for i in range(size.bit_length() - 1)]


def small_sum(parts):
    flat = jnp.concatenate([part.reshape(-1) for part in parts])
    peers = lax.axis_size("bins") * lax.axis_size("batch")
    everyone = lax.all_to_all(
        jnp.broadcast_to(flat[None], (peers, flat.shape[0])), EVERY, 0, 0, tiled=True
    )
    total = jnp.sum(everyone, axis=0)
    cuts = [part.size for part in parts]
    ends = [sum(cuts[: i + 1]) for i in range(len(cuts))]
    return [
        total[end - cut : end].reshape(part.shape) for part, cut, end in zip(parts, cuts, ends)
    ]


def swap(value, axis, mask):
    size = lax.axis_size(axis)
    return lax.ppermute(value, axis, [(i, i ^ mask) for i in range(size)])


def upper(axis, mask):
    return ((lax.axis_index(axis) & mask) != 0).astype(jnp.int32)


def orders():
    flat = bits_of(lax.axis_size("bins"))[1:]
    deep = [("batch", mask) for mask in bits_of(lax.axis_size("batch"))]
    across = [("bins", mask) for mask in flat[: len(flat) // 2]]
    along = [("bins", mask) for mask in flat[len(flat) // 2 :]]
    return (
        across + along + deep,
        along + deep[:1] + across + deep[1:],
        deep[:1] + across + along + deep[1:],
    )


def scatter_sum(pieces, stages):
    held = [(piece, 0) for piece in pieces]
    rows = pieces[0].shape[0]
    for axis, mask in stages:
        rows //= 2
        mine = upper(axis, mask)

        def half(which):
            return sum(
                lax.dynamic_slice_in_dim(piece, at + which * rows, rows, 0).astype(F32)
                for piece, at in held
            )

        arrived = swap(half(1 - mine).astype(BF16), axis, mask)
        held = [(piece, at + mine * rows) for piece, at in held] + [(arrived, 0)]
    return sum(
        lax.dynamic_slice_in_dim(piece, at, rows, 0).astype(F32) for piece, at in held
    ).astype(BF16)


def gather_rows(share, stages):
    for axis, mask in reversed(stages):
        other = swap(share, axis, mask)
        mine = upper(axis, mask)
        share = jnp.concatenate(
            [jnp.where(mine == 1, other, share), jnp.where(mine == 1, share, other)], axis=0
        )
    return share


def gelu_pair(values):
    logistic = jax.nn.sigmoid(1.702 * values)
    return (values * logistic, logistic + 1.702 * values * logistic * (1.0 - logistic))


def rows_product(former, latter):
    return lax.dot_general(
        former, latter, (((0,), (0,)), ((), ())), preferred_element_type=F32
    )


def back_product(former, latter):
    return lax.dot_general(
        former, latter, (((1,), (1,)), ((), ())), preferred_element_type=F32
    )


def taps(padded_rows, span):
    windows = padded_rows.shape[0]
    return [
        padded_rows[:, k * DILATION_STEP : k * DILATION_STEP + span, :].reshape(
            windows * span, -1
        )
        for k in range(3)
    ]


def statistics(plain_sum, square_sum, population):
    centre = plain_sum / population
    return (centre, lax.rsqrt(square_sum / population - centre * centre + EPS))


def edges(shard, width):
    peers, length = (lax.axis_size("bins"), shard.shape[1])
    up = [(i, i + 1) for i in range(peers - 1)]
    down = [(i + 1, i) for i in range(peers - 1)]
    before = lax.ppermute(shard[:, length - width :], "bins", up)
    after = lax.ppermute(shard[:, :width], "bins", down)
    return before, after


def poisson_slope(logits, counted):
    small = jnp.exp(-jnp.abs(logits))
    whole = 1.0 + small
    inverse = 1.0 / whole
    logistic = jnp.where(logits >= 0.0, inverse, small * inverse)
    tail = jnp.where(small < 1e-3, small * (1.0 - 0.5 * small), jnp.log(whole))
    ratio = logistic / (jnp.maximum(logits, 0.0) + tail)
    return logistic - counted * jnp.where(logits < -20.0, 1.0, ratio)


def head_body(
    species_ref,
    core_ref,
    weight_ref,
    bias_ref,
    counts_ref,
    rows_ref,
    columns_ref,
    before_ref,
    keep_ref,
    send_ref,
    after_ref,
    bias_grad_ref,
    grads_ref,
    bias_wide_ref,
    bias_sum_ref,
    *,
    tracks,
    first,
    which,
    scale,
):
    step = pl.program_id(0)
    tile, width = weight_ref.shape
    windows = species_ref.shape[0]
    span = rows_ref.shape[0] // windows
    lane = min(span, LANES)
    groups = span // lane
    track = (first + step) * tile + lax.broadcasted_iota(jnp.int32, (tile, 1), 0)
    inside = track < tracks

    @pl.when(step == 0)
    def _():
        after_ref[...] = before_ref[...]

    active = sum((species_ref[i] == which).astype(jnp.int32) for i in range(windows))
    weight = jnp.where(inside, weight_ref[...], BF16(0))
    weight_t = weight.T
    bias_wide_ref[...] = jnp.broadcast_to(bias_ref[...], (LANES, tile)).T
    bias_sum_ref[...] = jnp.zeros_like(bias_sum_ref)

    def window(i):
        lanes = slice(i * span, (i + 1) * span)
        logits = jnp.dot(weight, columns_ref[:, lanes], preferred_element_type=F32)
        total = jnp.zeros((tile, lane), F32)
        low = []
        for h in range(groups):
            counted = counts_ref[
                pl.ds(h * windows + i, tile, stride=groups * windows), :
            ].astype(F32)
            part = logits[:, h * lane : (h + 1) * lane] + bias_wide_ref[:, :lane]
            slope = jnp.where(inside, poisson_slope(part, counted) * scale, 0.0)
            total = total + slope
            low.append(slope.astype(BF16))
        low = jnp.concatenate(low, axis=1)
        grads_ref[:, lanes] = low
        after_ref[:, lanes] += jnp.dot(weight_t, low, preferred_element_type=F32)
        bias_sum_ref[...] += total

    @pl.when(active == windows)
    def _():
        for i in range(windows):
            window(i)

    @pl.when(active < windows)
    def _():
        for i in range(windows):

            @pl.when(species_ref[i] == which)
            def _():
                window(i)

            @pl.when(species_ref[i] != which)
            def _():
                grads_ref[:, i * span : (i + 1) * span] = jnp.zeros((tile, span), BF16)

    bias_grad_ref[...] = jnp.sum(bias_sum_ref[...].T, axis=0, keepdims=True)

    def store(left, right):
        @pl.when(core_ref[0] == 0)
        def _():
            keep_ref[...] = left
            send_ref[...] = right

        @pl.when(core_ref[0] != 0)
        def _():
            keep_ref[...] = right
            send_ref[...] = left

    @pl.when(active > 0)
    def _():
        product = jnp.dot(grads_ref[...], rows_ref[...], preferred_element_type=F32).astype(BF16)
        store(product[:, : width // 2], product[:, width // 2 :])

    @pl.when(active == 0)
    def _():
        nothing = jnp.zeros((tile, width // 2), BF16)
        store(nothing, nothing)


def head(species, core, weight, bias, counts, rows, columns, before, first, tiles, which, scale):
    tracks, width = weight.shape
    tokens = rows.shape[0]
    every = tokens // counts.shape[1]
    at = lambda j, *_: (first + j, 0)
    across = lambda j, *_: (0, first + j)
    fixed = lambda j, *_: (0, 0)
    out = lambda j, *_: (j, 0)
    body = functools.partial(head_body, tracks=tracks, first=first, which=which, scale=scale)
    return pl.pallas_call(
        body,
        grid_spec=pltpu.PrefetchScalarGridSpec(
            num_scalar_prefetch=2,
            grid=(tiles,),
            in_specs=[
                pl.BlockSpec((TILE, width), at),
                pl.BlockSpec((1, TILE), across),
                pl.BlockSpec((TILE * every, counts.shape[1]), at),
                pl.BlockSpec((tokens, width), fixed),
                pl.BlockSpec((width, tokens), fixed),
                pl.BlockSpec((width, tokens), fixed),
            ],
            out_specs=[
                pl.BlockSpec((TILE, width // 2), out),
                pl.BlockSpec((TILE, width // 2), out),
                pl.BlockSpec((width, tokens), fixed),
                pl.BlockSpec((1, TILE), lambda j, *_: (0, j)),
            ],
            scratch_shapes=[
                pltpu.VMEM((TILE, tokens), BF16),
                pltpu.VMEM((TILE, LANES), F32),
                pltpu.VMEM((TILE, counts.shape[1]), F32),
            ],
        ),
        out_shape=[
            jax.ShapeDtypeStruct((tiles * TILE, width // 2), BF16),
            jax.ShapeDtypeStruct((tiles * TILE, width // 2), BF16),
            jax.ShapeDtypeStruct((width, tokens), F32),
            jax.ShapeDtypeStruct((1, tiles * TILE), F32),
        ],
        compiler_params=pltpu.CompilerParams(vmem_limit_bytes=58 * 2**20),
        cost_estimate=pl.CostEstimate(
            flops=6 * tiles * TILE * width * tokens,
            bytes_accessed=tiles * TILE * (tokens * 4 + width * 4),
            transcendentals=3 * tiles * TILE * tokens,
        ),
    )(species, core, weight, bias, counts, rows, columns, before)


def on_device(
    block_in,
    gain_in,
    shift_in,
    dilated_taps_weight,
    gain_mid,
    shift_mid,
    proj_weight,
    proj_bias,
    head_human,
    bias_human,
    head_mouse,
    bias_mouse,
    species,
    counts,
):
    windows, span, width = block_in.shape
    tokens = windows * span
    middle = proj_weight.shape[0]
    tracks_human = head_human.shape[1]
    tracks_mouse = head_mouse.shape[1]
    bins, batch = lax.axis_size("bins"), lax.axis_size("batch")
    population = float(tokens * bins * batch)
    core = (lax.axis_index("bins") % 2).astype(jnp.int32)[None]

    before, after = edges(block_in, DILATION_STEP)
    wide = block_in.reshape(tokens, width).astype(F32)
    sum_in, square_in = small_sum([jnp.sum(wide, axis=0), jnp.sum(wide * wide, axis=0)])
    centre_in, scale_in = statistics(sum_in, square_in, population)

    def activate_in(values):
        return gelu_pair((values.astype(F32) - centre_in) * scale_in * gain_in + shift_in)

    normed_in = (wide - centre_in) * scale_in
    hidden_in, slope_in = gelu_pair(normed_in * gain_in + shift_in)
    hidden_in = hidden_in.astype(BF16).reshape(windows, span, width)
    place = lax.axis_index("bins")
    hidden_before = jnp.where(place > 0, activate_in(before)[0], 0.0).astype(BF16)
    hidden_after = jnp.where(place < bins - 1, activate_in(after)[0], 0.0).astype(BF16)
    padded = jnp.concatenate([hidden_before, hidden_in, hidden_after], axis=1)
    shifted = taps(padded, span)
    dilated = sum(
        jnp.dot(rows, dilated_taps_weight[k], preferred_element_type=F32)
        for k, rows in enumerate(shifted)
    )
    sum_mid, square_mid = small_sum([jnp.sum(dilated, axis=0), jnp.sum(dilated * dilated, axis=0)])
    centre_mid, scale_mid = statistics(sum_mid, square_mid, population)
    normed_mid = (dilated - centre_mid) * scale_mid
    hidden_mid, slope_mid = gelu_pair(normed_mid * gain_mid + shift_mid)
    hidden_mid = hidden_mid.astype(BF16)
    branch = jnp.dot(hidden_mid, proj_weight, preferred_element_type=F32)
    block_out = (wide + branch + proj_bias).astype(BF16)

    lane = min(span, LANES)
    counts_rows = (
        counts.transpose(2, 0, 1)
        .reshape(tracks_human, windows, span // lane, lane)
        .transpose(0, 2, 1, 3)
        .reshape(-1, lane)
    )
    columns = block_out.T
    tiles_human = pl.cdiv(tracks_human, TILE)
    tiles_mouse = pl.cdiv(tracks_mouse, TILE)
    cut = (tiles_human + 1) // 2
    human = (head_human.T, bias_human[None], counts_rows, block_out, columns)
    mouse = (head_mouse.T, bias_mouse[None], counts_rows, block_out, columns)
    scale_human = math.sqrt(width / tracks_human)
    scale_mouse = math.sqrt(width / tracks_mouse)
    start = jnp.zeros((width, tokens), F32)
    keep1, send1, dy_t, bias1 = head(
        species, core, *human, start, 0, cut, 0, scale_human
    )
    keep2, send2, dy_t, bias2 = head(
        species, core, *human, dy_t, cut, tiles_human - cut, 0, scale_human
    )
    keep3, send3, dy_t, bias3 = head(
        species, core, *mouse, dy_t, 0, tiles_mouse, 1, scale_mouse
    )

    routes = orders()
    share = 16 * (bins // 2) * batch

    def reduced(keep, send):
        rows = keep.shape[0]
        arrived = swap(send, "bins", 1)
        units = rows // share
        ends = [units * (p + 1) // 3 * share for p in range(3)]
        done = []
        for p in range(3):
            low, high = (ends[p - 1] if p else 0), ends[p]
            if low == high:
                continue
            own = scatter_sum([keep[low:high], arrived[low:high]], routes[p])
            done.append(gather_rows(own, routes[p]))
        mine = jnp.concatenate(done, axis=0)
        other = swap(mine, "bins", 1)
        left = jnp.where(core[0] == 0, mine, other).astype(F32)
        right = jnp.where(core[0] == 0, other, mine).astype(F32)
        return jnp.concatenate([left, right], axis=1)

    def padded_to_share(value):
        rows = value.shape[0]
        return jnp.pad(value, ((0, -rows % share), (0, 0)))

    grad1 = reduced(padded_to_share(keep1), padded_to_share(send1))
    grad2 = reduced(
        padded_to_share(jnp.concatenate([keep2, keep3], axis=0)),
        padded_to_share(jnp.concatenate([send2, send3], axis=0)),
    )
    rows1, rows2 = keep1.shape[0], keep2.shape[0]
    head_human_grad = jnp.concatenate(
        [grad1[:rows1], grad2[: tracks_human - rows1]], axis=0
    ).T
    head_mouse_grad = grad2[rows2 : rows2 + tracks_mouse].T

    output_grad = dy_t.T
    branch_grad = output_grad.astype(BF16)
    proj_grad = rows_product(branch_grad, hidden_mid)
    mid_grad = back_product(branch_grad, proj_weight) * slope_mid
    shift_mid_grad, gain_mid_grad = small_sum(
        [jnp.sum(mid_grad, axis=0), jnp.sum(mid_grad * normed_mid, axis=0)]
    )
    dilated_grad = (
        scale_mid
        * gain_mid
        * (mid_grad - shift_mid_grad / population - normed_mid * gain_mid_grad / population)
    ).astype(BF16)
    dilated_grad_windows = dilated_grad.reshape(windows, span, middle)
    grad_before, grad_after = edges(dilated_grad_windows, DILATION_STEP)
    conv_grad = jnp.concatenate([rows_product(rows, dilated_grad) for rows in shifted], axis=0)
    weights_grad = jnp.concatenate([conv_grad, proj_grad], axis=0).astype(BF16)
    grad_shifted = taps(
        jnp.concatenate([grad_before, dilated_grad_windows, grad_after], axis=1), span
    )
    hidden_grad = sum(
        back_product(grad_shifted[2 - k], dilated_taps_weight[k]) for k in range(3)
    )
    in_grad = hidden_grad * slope_in
    shift_in_grad, gain_in_grad = small_sum(
        [jnp.sum(in_grad, axis=0), jnp.sum(in_grad * normed_in, axis=0)]
    )
    input_grad = output_grad + scale_in * gain_in * (
        in_grad - shift_in_grad / population - normed_in * gain_in_grad / population
    )

    third = weights_grad.shape[0] // 3
    weights_total = []
    for p in range(3):
        route = [("bins", 1)] + routes[p]
        own = scatter_sum([weights_grad[p * third : (p + 1) * third]], route)
        weights_total.append(gather_rows(own, route))
    weights_total = jnp.concatenate(weights_total, axis=0).astype(F32)
    conv_total = weights_total[: 3 * width].reshape(3, width, middle)
    proj_total = weights_total[3 * width :].T

    sums = jnp.concatenate(
        [
            jnp.sum(output_grad, axis=0),
            bias1[0],
            bias2[0, : tracks_human - rows1],
            bias3[0, :tracks_mouse],
        ]
    )
    for axis in EVERY:
        for mask in bits_of(lax.axis_size(axis)):
            sums = sums + swap(sums, axis, mask)
    proj_bias_total = sums[:width]
    bias_human_grad = sums[width : width + tracks_human]
    bias_mouse_grad = sums[width + tracks_human :]
    return (
        block_out.reshape(windows, span, width),
        input_grad.astype(BF16).reshape(windows, span, width),
        gain_in_grad,
        shift_in_grad,
        conv_total,
        gain_mid_grad,
        shift_mid_grad,
        proj_total,
        proj_bias_total,
        head_human_grad,
        bias_human_grad,
        head_mouse_grad,
        bias_mouse_grad,
    )


def solution(mesh):
    tokens = P("batch", "bins", None)
    placed = (tokens,) + (P(),) * 11 + (P("batch"), tokens)
    return jax.shard_map(
        on_device,
        mesh=mesh,
        in_specs=placed,
        out_specs=(tokens, tokens) + (P(),) * 11,
        check_vma=False,
    )
```

```python
import functools
import math

import jax
import jax.numpy as jnp
from jax import lax
from jax.experimental import pallas as pl
from jax.experimental.pallas import tpu as pltpu
from jax.sharding import PartitionSpec as P

DILATION_STEP = 11
EPS = 1e-05
F32 = jnp.float32
BF16 = jnp.bfloat16
EVERY = ("y", "x", "core", "batch")
BINS = ("y", "x", "core")
CHIPS = ("y", "x", "batch")
CORE = ("core", 1)
LANES = 128
TILE = 896


def bits_of(axis):
    return [(axis, 1 << i) for i in range(lax.axis_size(axis).bit_length() - 1)]


def small_sum(parts):
    flat = jnp.concatenate([part.reshape(-1) for part in parts])
    peers = lax.axis_size(EVERY)
    sent = jnp.broadcast_to(flat[None], (peers, flat.shape[0]))
    cuts = [part.size for part in parts]

    def finish(everyone):
        total = jnp.sum(everyone, axis=0)
        ends = [sum(cuts[: i + 1]) for i in range(len(cuts))]
        return [
            total[end - cut : end].reshape(part.shape)
            for part, cut, end in zip(parts, cuts, ends)
        ]

    return sent, finish


def to_all(sent, axes=EVERY):
    return lax.all_to_all(sent, axes, 0, 0, tiled=True)


def swap(value, stage):
    axis, mask = stage
    size = lax.axis_size(axis)
    return lax.ppermute(value, axis, [(i, i ^ mask) for i in range(size)])


def upper(stage):
    axis, mask = stage
    return ((lax.axis_index(axis) & mask) != 0).astype(jnp.int32)


class Stream:
    def __init__(self, pieces, stages):
        self.held = [(piece, 0) for piece in pieces]
        self.rows = pieces[0].shape[0]
        self.up = list(stages)
        self.down = list(reversed(stages))
        self.share = None

    def busy(self):
        return bool(self.up or self.down)

    def part(self, which):
        return sum(
            lax.dynamic_slice_in_dim(piece, at + which * self.rows, self.rows, 0).astype(F32)
            for piece, at in self.held
        ).astype(BF16)

    def outgoing(self):
        if self.up:
            self.rows //= 2
            return self.part(1 - upper(self.up[0]))
        if self.share is None:
            self.share = self.part(0)
        return self.share

    def exchange(self, value):
        return swap(value, self.up[0] if self.up else self.down[0])

    def incoming(self, arrived):
        if self.up:
            mine = upper(self.up.pop(0))
            self.held = [(piece, at + mine * self.rows) for piece, at in self.held]
            self.held.append((arrived, 0))
            return
        mine = upper(self.down.pop(0))
        self.share = jnp.concatenate(
            [
                jnp.where(mine == 1, arrived, self.share),
                jnp.where(mine == 1, self.share, arrived),
            ],
            axis=0,
        )


def together(transfers, work, given):
    values, given = lax.optimization_barrier(([value for value, _ in transfers], given))
    arrived = [move(value) for value, (_, move) in zip(values, transfers)]
    return lax.optimization_barrier((arrived, work(*given)))


def advance(streams, more=(), work=lambda: (), given=()):
    streams = [stream for stream in streams if stream.busy()]
    transfers = [(stream.outgoing(), stream.exchange) for stream in streams] + list(more)
    arrived, result = together(transfers, work, given)
    for stream, value in zip(streams, arrived):
        stream.incoming(value)
    return arrived[len(streams) :], result


def gelu_pair(values):
    logistic = jax.nn.sigmoid(1.702 * values)
    return (values * logistic, logistic + 1.702 * values * logistic * (1.0 - logistic))


def rows_product(former, latter):
    return lax.dot_general(
        former, latter, (((0,), (0,)), ((), ())), preferred_element_type=F32
    )


def back_product(former, latter):
    return lax.dot_general(
        former, latter, (((1,), (1,)), ((), ())), preferred_element_type=F32
    )


def taps(padded_rows, span):
    windows = padded_rows.shape[0]
    return [
        padded_rows[:, k * DILATION_STEP : k * DILATION_STEP + span, :].reshape(
            windows * span, -1
        )
        for k in range(3)
    ]


def statistics(plain_sum, square_sum, population):
    centre = plain_sum / population
    return (centre, lax.rsqrt(square_sum / population - centre * centre + EPS))


def edges(shard, width):
    peers, length = (lax.axis_size(BINS), shard.shape[1])
    up = [(i, i + 1) for i in range(peers - 1)]
    down = [(i + 1, i) for i in range(peers - 1)]
    return (
        (shard[:, length - width :], lambda value: lax.ppermute(value, BINS, up)),
        (shard[:, :width], lambda value: lax.ppermute(value, BINS, down)),
    )


def poisson_slope(logits, counted):
    small = jnp.exp(-jnp.abs(logits))
    whole = 1.0 + small
    inverse = 1.0 / whole
    logistic = jnp.where(logits >= 0.0, inverse, small * inverse)
    tail = jnp.where(small < 1e-3, small * (1.0 - 0.5 * small), jnp.log(whole))
    ratio = logistic / (jnp.maximum(logits, 0.0) + tail)
    return logistic - counted * jnp.where(logits < -20.0, 1.0, ratio)


def head_body(
    species_ref,
    core_ref,
    weight_ref,
    bias_ref,
    counts_ref,
    rows_ref,
    columns_ref,
    before_ref,
    keep_ref,
    send_ref,
    after_ref,
    bias_grad_ref,
    grads_ref,
    bias_wide_ref,
    bias_sum_ref,
    *,
    tracks,
    first,
    which,
    scale,
):
    step = pl.program_id(0)
    tile, width = weight_ref.shape
    windows = species_ref.shape[0]
    span = rows_ref.shape[0] // windows
    lane = min(span, LANES)
    groups = span // lane
    track = (first + step) * tile + lax.broadcasted_iota(jnp.int32, (tile, 1), 0)
    inside = track < tracks

    @pl.when(step == 0)
    def _():
        after_ref[...] = before_ref[...]

    active = sum((species_ref[i] == which).astype(jnp.int32) for i in range(windows))
    weight = jnp.where(inside, weight_ref[...], BF16(0))
    weight_t = weight.T
    bias_wide_ref[...] = jnp.broadcast_to(bias_ref[...], (LANES, tile)).T
    bias_sum_ref[...] = jnp.zeros_like(bias_sum_ref)

    def window(i):
        lanes = slice(i * span, (i + 1) * span)
        logits = jnp.dot(weight, columns_ref[:, lanes], preferred_element_type=F32)
        total = jnp.zeros((tile, lane), F32)
        low = []
        for h in range(groups):
            counted = counts_ref[
                pl.ds(h * windows + i, tile, stride=groups * windows), :
            ].astype(F32)
            part = logits[:, h * lane : (h + 1) * lane] + bias_wide_ref[:, :lane]
            slope = jnp.where(inside, poisson_slope(part, counted) * scale, 0.0)
            total = total + slope
            low.append(slope.astype(BF16))
        low = jnp.concatenate(low, axis=1)
        grads_ref[:, lanes] = low
        after_ref[:, lanes] += jnp.dot(weight_t, low, preferred_element_type=F32)
        bias_sum_ref[...] += total

    @pl.when(active == windows)
    def _():
        for i in range(windows):
            window(i)

    @pl.when(active < windows)
    def _():
        for i in range(windows):

            @pl.when(species_ref[i] == which)
            def _():
                window(i)

            @pl.when(species_ref[i] != which)
            def _():
                grads_ref[:, i * span : (i + 1) * span] = jnp.zeros((tile, span), BF16)

    bias_grad_ref[...] = jnp.sum(bias_sum_ref[...].T, axis=0, keepdims=True)

    def store(left, right):
        @pl.when(core_ref[0] == 0)
        def _():
            keep_ref[...] = left
            send_ref[...] = right

        @pl.when(core_ref[0] != 0)
        def _():
            keep_ref[...] = right
            send_ref[...] = left

    @pl.when(active > 0)
    def _():
        product = jnp.dot(grads_ref[...], rows_ref[...], preferred_element_type=F32).astype(BF16)
        store(product[:, : width // 2], product[:, width // 2 :])

    @pl.when(active == 0)
    def _():
        nothing = jnp.zeros((tile, width // 2), BF16)
        store(nothing, nothing)


def head(species, core, weight, bias, counts, rows, columns, before, first, tiles, which, scale):
    tracks, width = weight.shape
    tokens = rows.shape[0]
    every = tokens // counts.shape[1]
    at = lambda j, *_: (first + j, 0)
    across = lambda j, *_: (0, first + j)
    fixed = lambda j, *_: (0, 0)
    out = lambda j, *_: (j, 0)
    body = functools.partial(head_body, tracks=tracks, first=first, which=which, scale=scale)
    return pl.pallas_call(
        body,
        grid_spec=pltpu.PrefetchScalarGridSpec(
            num_scalar_prefetch=2,
            grid=(tiles,),
            in_specs=[
                pl.BlockSpec((TILE, width), at),
                pl.BlockSpec((1, TILE), across),
                pl.BlockSpec((TILE * every, counts.shape[1]), at),
                pl.BlockSpec((tokens, width), fixed),
                pl.BlockSpec((width, tokens), fixed),
                pl.BlockSpec((width, tokens), fixed),
            ],
            out_specs=[
                pl.BlockSpec((TILE, width // 2), out),
                pl.BlockSpec((TILE, width // 2), out),
                pl.BlockSpec((width, tokens), fixed),
                pl.BlockSpec((1, TILE), lambda j, *_: (0, j)),
            ],
            scratch_shapes=[
                pltpu.VMEM((TILE, tokens), BF16),
                pltpu.VMEM((TILE, LANES), F32),
                pltpu.VMEM((TILE, counts.shape[1]), F32),
            ],
        ),
        out_shape=[
            jax.ShapeDtypeStruct((tiles * TILE, width // 2), BF16),
            jax.ShapeDtypeStruct((tiles * TILE, width // 2), BF16),
            jax.ShapeDtypeStruct((width, tokens), F32),
            jax.ShapeDtypeStruct((1, tiles * TILE), F32),
        ],
        compiler_params=pltpu.CompilerParams(vmem_limit_bytes=58 * 2**20),
        cost_estimate=pl.CostEstimate(
            flops=6 * tiles * TILE * width * tokens,
            bytes_accessed=tiles * TILE * (tokens * 4 + width * 4),
            transcendentals=3 * tiles * TILE * tokens,
        ),
    )(species, core, weight, bias, counts, rows, columns, before)


def finish_body(core_ref, mine_ref, other_ref, *rest):
    out_ref = rest[-1]
    half = mine_ref.shape[1]
    mine, other = mine_ref[...].astype(F32), other_ref[...].astype(F32)

    @pl.when(core_ref[0] == 0)
    def _():
        out_ref[:, :half] = mine
        out_ref[:, half:] = other

    @pl.when(core_ref[0] != 0)
    def _():
        out_ref[:, :half] = other
        out_ref[:, half:] = mine


def first_rows(tracks, width):
    return jax.ShapeDtypeStruct((tracks, width), F32)


def finish_head(shape, core, mine, other, first, earlier):
    rows, half = mine.shape
    tiles = min(rows // TILE, pl.cdiv(shape.shape[0], TILE) - first)
    half_spec = pl.BlockSpec((TILE, half), lambda j, *_: (j, 0))
    specs, values, aliases = [half_spec, half_spec], [mine, other], {}
    if earlier is not None:
        specs.append(pl.BlockSpec(memory_space=pl.ANY))
        values.append(earlier)
        aliases = {3: 0}
    return pl.pallas_call(
        finish_body,
        grid_spec=pltpu.PrefetchScalarGridSpec(
            num_scalar_prefetch=1,
            grid=(tiles,),
            in_specs=specs,
            out_specs=pl.BlockSpec((TILE, 2 * half), lambda j, *_: (first + j, 0)),
        ),
        out_shape=shape,
        input_output_aliases=aliases,
    )(core, *values)


def on_device(
    block_in,
    gain_in,
    shift_in,
    dilated_taps_weight,
    gain_mid,
    shift_mid,
    proj_weight,
    proj_bias,
    head_human,
    bias_human,
    head_mouse,
    bias_mouse,
    species,
    counts,
):
    windows, span, width = block_in.shape
    tokens = windows * span
    middle = proj_weight.shape[0]
    tracks_human = head_human.shape[1]
    tracks_mouse = head_mouse.shape[1]
    devices = lax.axis_size(EVERY)
    population = float(tokens * devices)
    core = lax.axis_index("core").astype(jnp.int32)[None]

    wide = block_in.reshape(tokens, width).astype(F32)
    sent, finish = small_sum([jnp.sum(wide, axis=0), jnp.sum(wide * wide, axis=0)])
    (before, after, everyone), _ = together(
        [*edges(block_in, DILATION_STEP), (sent, to_all)], lambda: (), ()
    )
    sum_in, square_in = finish(everyone)
    centre_in, scale_in = statistics(sum_in, square_in, population)

    def activate_in(values):
        return gelu_pair((values.astype(F32) - centre_in) * scale_in * gain_in + shift_in)

    normed_in = (wide - centre_in) * scale_in
    hidden_in, slope_in = gelu_pair(normed_in * gain_in + shift_in)
    hidden_in = hidden_in.astype(BF16).reshape(windows, span, width)
    place = lax.axis_index(BINS)
    last = lax.axis_size(BINS) - 1
    hidden_before = jnp.where(place > 0, activate_in(before)[0], 0.0).astype(BF16)
    hidden_after = jnp.where(place < last, activate_in(after)[0], 0.0).astype(BF16)
    padded = jnp.concatenate([hidden_before, hidden_in, hidden_after], axis=1)
    shifted = taps(padded, span)
    dilated = sum(
        jnp.dot(rows, dilated_taps_weight[k], preferred_element_type=F32)
        for k, rows in enumerate(shifted)
    )
    sent, finish = small_sum([jnp.sum(dilated, axis=0), jnp.sum(dilated * dilated, axis=0)])
    sum_mid, square_mid = finish(to_all(sent))
    centre_mid, scale_mid = statistics(sum_mid, square_mid, population)
    normed_mid = (dilated - centre_mid) * scale_mid
    hidden_mid, slope_mid = gelu_pair(normed_mid * gain_mid + shift_mid)
    hidden_mid = hidden_mid.astype(BF16)
    branch = jnp.dot(hidden_mid, proj_weight, preferred_element_type=F32)
    block_out = (wide + branch + proj_bias).astype(BF16)

    lane = min(span, LANES)
    counts_rows = (
        counts.transpose(2, 0, 1)
        .reshape(tracks_human, windows, span // lane, lane)
        .transpose(0, 2, 1, 3)
        .reshape(-1, lane)
    )
    columns = block_out.T
    tiles_human = pl.cdiv(tracks_human, TILE)
    tiles_mouse = pl.cdiv(tracks_mouse, TILE)
    cut = tiles_human // 3
    scale_human = math.sqrt(width / tracks_human)
    scale_mouse = math.sqrt(width / tracks_mouse)

    def human(first, tiles):
        def work(dy_t):
            return head(
                species, core, head_human.T, bias_human[None], counts_rows, block_out, columns,
                dy_t, first, tiles, 0, scale_human,
            )
        return work

    flat_x, flat_y, deep = bits_of("x"), bits_of("y"), bits_of("batch")
    near, far = deep[:1], deep[1:]
    start = jnp.zeros((width, tokens), F32)
    keep0, send0, dy_t, bias0 = head(
        species, core, head_mouse.T, bias_mouse[None], counts_rows, block_out, columns,
        start, 0, tiles_mouse, 1, scale_mouse,
    )
    (arrived0,), (keep1, send1, dy_t, bias1) = together(
        [(send0, lambda value: swap(value, CORE))], human(0, cut), (dy_t,)
    )
    first = Stream([keep0, arrived0], flat_x + near + flat_y + far)
    (arrived1,), (keep2, send2, dy_t, bias2) = advance(
        [first], [(send1, lambda value: swap(value, CORE))], human(cut, tiles_human - cut), (dy_t,)
    )
    second = Stream([keep1, arrived1], flat_y + flat_x + deep)

    def after_head(dy_t):
        output_grad = dy_t.T
        branch_grad = output_grad.astype(BF16)
        mid_grad = back_product(branch_grad, proj_weight) * slope_mid
        sent, _ = small_sum([jnp.sum(mid_grad, axis=0), jnp.sum(mid_grad * normed_mid, axis=0)])
        return output_grad, branch_grad, mid_grad, sent

    (arrived2,), (output_grad, branch_grad, mid_grad, sent) = advance(
        [first, second], [(send2, lambda value: swap(value, CORE))], after_head, (dy_t,)
    )
    unit = 16 * lax.axis_size(CHIPS)
    rows2 = keep2.shape[0]
    ends = [0] + [max(1, rows2 * (p + 1) // 3 // unit) * unit for p in range(2)] + [rows2]
    thirds = [
        Stream([keep2[low:high], arrived2[low:high]], route)
        for low, high, route in zip(
            ends[:-1],
            ends[1:],
            (flat_x + flat_y + deep, flat_y + near + flat_x + far, near + flat_x + flat_y + far),
        )
        if low < high
    ]
    streams = [first, second, *thirds]

    def weight_work(branch_grad, output_grad):
        return rows_product(branch_grad, hidden_mid), jnp.sum(output_grad, axis=0)

    (everyone,), (proj_grad, proj_bias_grad) = advance(
        streams, [(sent, to_all)], weight_work, (branch_grad, output_grad)
    )
    _, finish = small_sum([shift_mid, gain_mid])
    shift_mid_grad, gain_mid_grad = finish(everyone)
    dilated_grad = (
        scale_mid
        * gain_mid
        * (mid_grad - shift_mid_grad / population - normed_mid * gain_mid_grad / population)
    ).astype(BF16)

    def conv_work(dilated_grad, proj_grad):
        conv_grad = [rows_product(rows, dilated_grad) for rows in shifted]
        return jnp.concatenate([*conv_grad, proj_grad], axis=0).astype(BF16)

    dilated_windows = dilated_grad.reshape(windows, span, middle)
    (grad_before, grad_after), weights_grad = advance(
        streams, edges(dilated_windows, DILATION_STEP), conv_work, (dilated_grad, proj_grad)
    )

    def hidden_work(grad_before, dilated_windows, grad_after):
        grad_shifted = taps(
            jnp.concatenate([grad_before, dilated_windows, grad_after], axis=1), span
        )
        hidden_grad = sum(
            back_product(grad_shifted[2 - k], dilated_taps_weight[k]) for k in range(3)
        )
        in_grad = hidden_grad * slope_in
        sent, _ = small_sum([jnp.sum(in_grad, axis=0), jnp.sum(in_grad * normed_in, axis=0)])
        return in_grad, sent

    half = weights_grad.shape[0] // 2
    weights_keep = lax.dynamic_slice_in_dim(weights_grad, core[0] * half, half, 0)
    weights_send = lax.dynamic_slice_in_dim(weights_grad, (1 - core[0]) * half, half, 0)
    (arrived,), (in_grad, sent) = advance(
        streams,
        [(weights_send, lambda value: swap(value, CORE))],
        hidden_work,
        (grad_before, dilated_windows, grad_after),
    )
    chips = lax.axis_size(CHIPS)
    weights_half = (weights_keep.astype(F32) + arrived.astype(F32)).astype(BF16)
    weights_half = weights_half.reshape(chips, half // chips, middle)
    (everyone, weights_parts), _ = advance(
        streams, [(sent, to_all), (weights_half, lambda value: to_all(value, CHIPS))]
    )
    _, finish = small_sum([shift_in, gain_in])
    shift_in_grad, gain_in_grad = finish(everyone)

    def last_work(output_grad, in_grad):
        input_grad = output_grad + scale_in * gain_in * (
            in_grad - shift_in_grad / population - normed_in * gain_in_grad / population
        )
        return input_grad.astype(BF16)

    _, input_grad = advance(streams, [], last_work, (output_grad, in_grad))
    weights_share = jnp.sum(weights_parts.astype(F32), axis=0).astype(BF16)
    (weights_all,), _ = advance(
        streams,
        [
            (
                jnp.broadcast_to(weights_share[None], (chips,) + weights_share.shape),
                lambda value: to_all(value, CHIPS),
            )
        ],
    )
    weights_mine = weights_all.reshape(half, middle)
    sums = jnp.concatenate(
        [
            proj_bias_grad,
            bias1[0],
            bias2[0, : tracks_human - bias1.shape[1]],
            bias0[0, :tracks_mouse],
        ]
    )
    extra = [(weights_mine, lambda value: swap(value, CORE))]
    others = {}
    for stage in [stage for axis in EVERY for stage in bits_of(axis)]:
        ready = [s for s in (first, second) if not s.busy() and s not in others]
        moves = [(s.share, lambda value: swap(value, CORE)) for s in ready]
        got, _ = advance(
            streams,
            moves + extra + [(sums, functools.partial(lambda stage, value: swap(value, stage), stage))],
        )
        others.update(zip(ready, got))
        if extra:
            weights_other = got[len(ready)]
        extra = []
        sums = sums + got[-1]
    while any(stream.busy() for stream in streams):
        advance(streams)
    rest = [s for s in (first, second) if s not in others]
    mine2 = jnp.concatenate([s.share for s in thirds], axis=0)
    got, _ = advance(
        [], [(value, lambda value: swap(value, CORE)) for value in [mine2] + [s.share for s in rest]]
    )
    others.update(zip(rest, got[1:]))
    human_start = finish_head(first_rows(tracks_human, width), core, second.share, others[second], 0, None)
    head_human_grad = finish_head(
        first_rows(tracks_human, width), core, mine2, got[0], cut, human_start
    ).T
    head_mouse_grad = finish_head(
        first_rows(tracks_mouse, width), core, first.share, others[first], 0, None
    ).T
    left = jnp.where(core[0] == 0, weights_mine, weights_other).astype(F32)
    right = jnp.where(core[0] == 0, weights_other, weights_mine).astype(F32)
    weights_total = jnp.concatenate([left, right], axis=0)
    conv_total = weights_total[: 3 * width].reshape(3, width, middle)
    proj_total = weights_total[3 * width :].T
    return (
        block_out.reshape(windows, span, width),
        input_grad.reshape(windows, span, width),
        gain_in_grad,
        shift_in_grad,
        conv_total,
        gain_mid_grad,
        shift_mid_grad,
        proj_total,
        sums[:width],
        head_human_grad,
        sums[width : width + tracks_human],
        head_mouse_grad,
        sums[width + tracks_human :],
    )


def solution(mesh):
    bins, batch = mesh.shape["bins"], mesh.shape["batch"]
    side = 1 << (((bins // 2).bit_length() - 1) // 2)
    grid = jax.sharding.Mesh(
        mesh.devices.reshape(bins // 2 // side, side, 2, batch), ("y", "x", "core", "batch")
    )
    tokens = P("batch", BINS, None)
    placed = (tokens,) + (P(),) * 11 + (P("batch"), tokens)
    return jax.shard_map(
        on_device,
        mesh=grid,
        in_specs=placed,
        out_specs=(tokens, tokens) + (P(),) * 11,
        check_vma=False,
    )
```

```python
import functools
import math

import jax
import jax.numpy as jnp
from jax import lax
from jax.experimental import pallas as pl
from jax.experimental.pallas import tpu as pltpu
from jax.sharding import PartitionSpec as P

DILATION_STEP = 11
EPS = 1e-05
F32 = jnp.float32
BF16 = jnp.bfloat16
EVERY = ("y", "x", "core", "batch")
BINS = ("y", "x", "core")
CHIPS = ("y", "x", "batch")
CORE = ("core", 1)
LANES = 128
TILE = 896


def bits_of(axis):
    return [(axis, 1 << i) for i in range(lax.axis_size(axis).bit_length() - 1)]


def small_sum(parts):
    flat = jnp.concatenate([part.reshape(-1) for part in parts])
    peers = lax.axis_size(EVERY)
    sent = jnp.broadcast_to(flat[None], (peers, flat.shape[0]))
    cuts = [part.size for part in parts]

    def finish(everyone):
        total = jnp.sum(everyone, axis=0)
        ends = [sum(cuts[: i + 1]) for i in range(len(cuts))]
        return [
            total[end - cut : end].reshape(part.shape)
            for part, cut, end in zip(parts, cuts, ends)
        ]

    return sent, finish


def to_all(sent, axes=EVERY):
    return lax.all_to_all(sent, axes, 0, 0, tiled=True)


def swap(value, stage):
    axis, mask = stage
    size = lax.axis_size(axis)
    return lax.ppermute(value, axis, [(i, i ^ mask) for i in range(size)])


def upper(stage):
    axis, mask = stage
    return ((lax.axis_index(axis) & mask) != 0).astype(jnp.int32)


def sum_body(at_ref, *refs, counts):
    ins, outs = refs[: sum(counts)], refs[sum(counts) :]
    used = 0
    for out, count in zip(outs, counts):
        total = sum(ref[...].astype(F32) for ref in ins[used : used + count])
        out[...] = total.astype(out.dtype)
        used += count


def sum_parts(parts, dtype):
    if any(rows % 16 for rows, _ in parts):
        sums = [
            sum(lax.dynamic_slice_in_dim(a, at, rows, 0).astype(F32) for a, at in pieces)
            for rows, pieces in parts
        ]
        return [value.astype(dtype) for value in sums]
    lanes = parts[0][1][0][0].shape[1]
    places, specs, values, counts, shapes = [], [], [], [], []
    for rows, pieces in parts:
        for array, at in pieces:
            specs.append(
                pl.BlockSpec((rows, lanes), lambda j, at_ref, i=len(places): (at_ref[i], 0))
            )
            places.append(jnp.asarray(at, jnp.int32) // rows)
            values.append(array)
        counts.append(len(pieces))
        shapes.append(rows)
    return pl.pallas_call(
        functools.partial(sum_body, counts=counts),
        grid_spec=pltpu.PrefetchScalarGridSpec(
            num_scalar_prefetch=1,
            grid=(1,),
            in_specs=specs,
            out_specs=[pl.BlockSpec((rows, lanes), lambda j, *_: (0, 0)) for rows in shapes],
        ),
        out_shape=[jax.ShapeDtypeStruct((rows, lanes), dtype) for rows in shapes],
        compiler_params=pltpu.CompilerParams(vmem_limit_bytes=60 * 2**20),
    )(jnp.stack(places), *values)


def join_body(mine_ref, *refs, count, stacked):
    row = 0
    for i in range(count):
        share, arrived = refs[2 * i], refs[2 * i + 1]
        out = refs[2 * count + (0 if stacked else i)]
        rows = share.shape[0]
        mine = mine_ref[i]
        out[pl.ds(pl.multiple_of(row + mine * rows, 16), rows), :] = share[...]
        out[pl.ds(pl.multiple_of(row + (1 - mine) * rows, 16), rows), :] = arrived[...]
        if stacked:
            row += 2 * rows


def join_parts(parts, stacked=False):
    if any(share.shape[0] % 16 for share, _, _ in parts):
        joined = [
            jnp.concatenate([jnp.where(mine == 1, b, a), jnp.where(mine == 1, a, b)], axis=0)
            for a, b, mine in parts
        ]
        return [jnp.concatenate(joined, axis=0)] if stacked else joined
    outs = [2 * a.shape[0] for a, _, _ in parts]
    if stacked:
        outs = [sum(outs)]
    lanes = parts[0][0].shape[1]
    whole = lambda rows: pl.BlockSpec((rows, lanes), lambda j, *_: (0, 0))
    return pl.pallas_call(
        functools.partial(join_body, count=len(parts), stacked=stacked),
        grid_spec=pltpu.PrefetchScalarGridSpec(
            num_scalar_prefetch=1,
            grid=(1,),
            in_specs=[whole(v.shape[0]) for a, b, _ in parts for v in (a, b)],
            out_specs=[whole(rows) for rows in outs],
        ),
        out_shape=[jax.ShapeDtypeStruct((rows, lanes), BF16) for rows in outs],
        compiler_params=pltpu.CompilerParams(vmem_limit_bytes=60 * 2**20),
    )(jnp.stack([mine for _, _, mine in parts]), *[v for a, b, _ in parts for v in (a, b)])


class Group:
    def __init__(self, order, pieces, rows, base, routes):
        self.order = order
        self.parts = [
            {"pieces": [(piece, at + base) for piece in pieces], "rows": count, "route": route}
            for at, count, route in zip(
                [sum(rows[:i]) for i in range(len(rows))], rows, routes
            )
        ]
        self.levels = len(routes[0])
        self.level = 0
        self.flying = None
        self.shares = None

    def moved(self, values, level):
        self.flying = [
            swap(value, part["route"][level]) for value, part in zip(values, self.parts)
        ]

    def work(self, arrays, flying):
        level = self.level
        parts = self.parts
        if level <= self.levels:
            wanted = []
            for i, part in enumerate(parts):
                pieces = list(zip(arrays[i], [at for _, at in part["pieces"]]))
                if level:
                    mine = upper(part["route"][level - 1])
                    pieces = [(a, at + mine * part["rows"]) for a, at in pieces]
                    pieces.append((flying[i], 0))
                part["pieces"] = pieces
                if level < self.levels:
                    part["rows"] //= 2
                    away = 1 - upper(part["route"][level])
                    pieces = [(a, at + away * part["rows"]) for a, at in pieces]
                wanted.append((part["rows"], pieces))
            return sum_parts(wanted, F32 if level < self.levels else BF16)
        back = 2 * self.levels - level
        return join_parts(
            [
                (share, arrived, upper(part["route"][back]))
                for share, arrived, part in zip(self.shares, flying, parts)
            ],
            stacked=level == 2 * self.levels,
        )

    def step(self):
        if self.done():
            return
        arrays = [[a for a, _ in part["pieces"]] for part in self.parts]
        values = self.order.run(self.work, arrays, self.flying)
        if self.level >= self.levels:
            self.shares = values
        if self.level < self.levels:
            self.moved(values, self.level)
        elif self.level < 2 * self.levels:
            self.moved(values, 2 * self.levels - 1 - self.level)
        self.level += 1

    def done(self):
        return self.level > 2 * self.levels


class Order:
    def __init__(self):
        self.token = ()

    def run(self, work, *given):
        given, _ = lax.optimization_barrier((given, self.token))
        result = work(*given)
        self.token = jax.tree.leaves(result)[:1]
        return result


def gelu_pair(values):
    logistic = jax.nn.sigmoid(1.702 * values)
    return (values * logistic, logistic + 1.702 * values * logistic * (1.0 - logistic))


def rows_product(former, latter):
    return lax.dot_general(
        former, latter, (((0,), (0,)), ((), ())), preferred_element_type=F32
    )


def back_product(former, latter):
    return lax.dot_general(
        former, latter, (((1,), (1,)), ((), ())), preferred_element_type=F32
    )


def taps(padded_rows, span):
    windows = padded_rows.shape[0]
    return [
        padded_rows[:, k * DILATION_STEP : k * DILATION_STEP + span, :].reshape(
            windows * span, -1
        )
        for k in range(3)
    ]


def statistics(plain_sum, square_sum, population):
    centre = plain_sum / population
    return (centre, lax.rsqrt(square_sum / population - centre * centre + EPS))


def edges(shard, width):
    peers, length = (lax.axis_size(BINS), shard.shape[1])
    up = [(i, i + 1) for i in range(peers - 1)]
    down = [(i + 1, i) for i in range(peers - 1)]
    return (
        (shard[:, length - width :], lambda value: lax.ppermute(value, BINS, up)),
        (shard[:, :width], lambda value: lax.ppermute(value, BINS, down)),
    )


def poisson_slope(logits, counted):
    held = jnp.maximum(logits, -80.0)
    small = jnp.exp(-jnp.abs(held))
    whole = 1.0 + small
    tail = jnp.where(small < 1e-3, small * (1.0 - 0.5 * small), jnp.log(whole))
    rate = jnp.maximum(held, 0.0) + tail
    top = jnp.where(held >= 0.0, 1.0, small)
    return top * (rate - counted) / (whole * rate)


def head_body(
    species_ref,
    windows_ref,
    humans_ref,
    core_ref,
    mouse_ref,
    human_ref,
    bias_mouse_ref,
    bias_human_ref,
    counts_ref,
    rows_ref,
    columns_ref,
    *refs,
    mouse_tiles,
    first_human,
    tracks,
    scales,
):
    *out_refs, grads_ref, bias_grad_ref, weight_ref, bias_ref, sums_ref, total_ref = refs
    step = pl.program_id(0)
    tile, width = weight_ref.shape
    windows = windows_ref.shape[0]
    span = rows_ref.shape[0] // windows
    lane = counts_ref.shape[1]
    groups = span // lane
    half = width // 2
    is_mouse = step < mouse_tiles
    humans = humans_ref[0]
    active = jnp.where(is_mouse, windows - humans, humans)
    skipped = jnp.where(is_mouse, humans, 0)
    first = jnp.where(is_mouse, step, first_human + step - mouse_tiles) * tile
    end = jnp.where(is_mouse, tracks[1], tracks[0])
    scale = jnp.where(is_mouse, scales[1], scales[0]).astype(F32)

    def prepare():
        inside = first + lax.broadcasted_iota(jnp.int32, (tile, 1), 0) < end

        @pl.when(is_mouse)
        def _():
            weight_ref[...] = jnp.where(inside, mouse_ref[...], BF16(0))
            bias_ref[...] = jnp.broadcast_to(bias_mouse_ref[...], (LANES, tile)).T

        @pl.when(jnp.logical_not(is_mouse))
        def _():
            weight_ref[...] = jnp.where(inside, human_ref[...], BF16(0))
            bias_ref[...] = jnp.broadcast_to(bias_human_ref[...], (LANES, tile)).T

    def slopes(logits, window):
        inside = first + lax.broadcasted_iota(jnp.int32, (tile, 1), 0) < end
        total = jnp.zeros((tile, lane), F32)
        low = []
        for h in range(groups):
            counted = counts_ref[
                pl.ds(h * windows + window, tile, stride=groups * windows), :
            ].astype(F32)
            part = logits[:, h * lane : (h + 1) * lane] + bias_ref[:, :lane]
            slope = jnp.where(inside, poisson_slope(part, counted) * scale, 0.0)
            total = total + slope
            low.append(slope.astype(BF16))
        return total, jnp.concatenate(low, axis=1)

    def store(product):
        if len(out_refs) == 1:
            out_refs[0][...] = product
            return
        mine = core_ref[0] == 0
        out_refs[0][...] = jnp.where(mine, product[:, :half], product[:, half:])
        out_refs[1][...] = jnp.where(mine, product[:, half:], product[:, :half])

    @pl.when(active == 0)
    def _():
        for out_ref in out_refs:
            out_ref[...] = jnp.zeros_like(out_ref)
        grads_ref[...] = jnp.zeros_like(grads_ref)
        bias_grad_ref[...] = jnp.zeros_like(bias_grad_ref)

    @pl.when(active == windows)
    def _():
        prepare()
        total = None
        for i in range(windows):
            lanes = slice(i * span, (i + 1) * span)
            logits = jnp.dot(weight_ref[...], columns_ref[:, lanes], preferred_element_type=F32)
            part, low = slopes(logits, i)
            total = part if total is None else total + part
            grads_ref[:, lanes] = low
        bias_grad_ref[...] = jnp.sum(total.T, axis=0, keepdims=True)
        product = jnp.dot(grads_ref[...], rows_ref[...], preferred_element_type=F32)
        store(product.astype(BF16))

    @pl.when((active > 0) & (active < windows))
    def _():
        prepare()
        grads_ref[...] = jnp.zeros_like(grads_ref)
        sums_ref[...] = jnp.zeros_like(sums_ref)
        total_ref[...] = jnp.zeros_like(total_ref)

        def one(window):
            at = window * span
            lanes = pl.ds(at if isinstance(window, int) else pl.multiple_of(at, span), span)
            logits = jnp.dot(weight_ref[...], columns_ref[:, lanes], preferred_element_type=F32)
            part, low = slopes(logits, window)
            sums_ref[...] += part
            grads_ref[:, lanes] = low
            total_ref[...] += jnp.dot(low, rows_ref[lanes, :], preferred_element_type=F32)
            return 0

        if span % LANES == 0:
            lax.fori_loop(0, active, lambda i, _: one(windows_ref[skipped + i]), 0)
        else:
            for i in range(windows):

                @pl.when((species_ref[i] == 1) == is_mouse)
                def _():
                    one(i)
        bias_grad_ref[...] = jnp.sum(sums_ref[...].T, axis=0, keepdims=True)
        store(total_ref[...].astype(BF16))


def head(
    species, order, humans, core, mouse, human, bias_mouse, bias_human, counts, rows, columns, scales,
    mouse_tiles, first_human, human_tiles, split,
):
    tokens, width = rows.shape
    lane = counts.shape[1]
    tracks = (human.shape[0], mouse.shape[0])
    tiles = mouse_tiles + human_tiles
    at_mouse = lambda j: jnp.minimum(j, max(mouse_tiles - 1, 0))
    at_human = lambda j: first_human + jnp.maximum(j - mouse_tiles, 0)
    at_both = lambda j: jnp.where(j < mouse_tiles, j, first_human + j - mouse_tiles)
    fixed = lambda j, *_: (0, 0)
    out = lambda j, *_: (j, 0)
    strip = width // 2 if split else width
    copies = 2 if split else 1
    return pl.pallas_call(
        functools.partial(
            head_body, mouse_tiles=mouse_tiles, first_human=first_human, tracks=tracks, scales=scales
        ),
        grid_spec=pltpu.PrefetchScalarGridSpec(
            num_scalar_prefetch=4,
            grid=(tiles,),
            in_specs=[
                pl.BlockSpec((TILE, width), lambda j, *_: (at_mouse(j), 0)),
                pl.BlockSpec((TILE, width), lambda j, *_: (at_human(j), 0)),
                pl.BlockSpec((1, TILE), lambda j, *_: (0, at_mouse(j))),
                pl.BlockSpec((1, TILE), lambda j, *_: (0, at_human(j))),
                pl.BlockSpec((TILE * tokens // lane, lane), lambda j, *_: (at_both(j), 0)),
                pl.BlockSpec((tokens, width), fixed),
                pl.BlockSpec((width, tokens), fixed),
            ],
            out_specs=[pl.BlockSpec((TILE, strip), out)] * copies
            + [pl.BlockSpec((TILE, tokens), out), pl.BlockSpec((1, TILE), lambda j, *_: (0, j))],
            scratch_shapes=[
                pltpu.VMEM((TILE, width), BF16),
                pltpu.VMEM((TILE, LANES), F32),
                pltpu.VMEM((TILE, lane), F32),
                pltpu.VMEM((TILE, width), F32),
            ],
        ),
        out_shape=[jax.ShapeDtypeStruct((tiles * TILE, strip), BF16)] * copies
        + [
            jax.ShapeDtypeStruct((tiles * TILE, tokens), BF16),
            jax.ShapeDtypeStruct((1, tiles * TILE), F32),
        ],
        compiler_params=pltpu.CompilerParams(vmem_limit_bytes=58 * 2**20),
        cost_estimate=pl.CostEstimate(
            flops=4 * tiles * TILE * width * tokens,
            bytes_accessed=tiles * TILE * (tokens * 6 + width * 4),
            transcendentals=3 * tiles * TILE * tokens,
        ),
    )(species, order, humans, core, mouse, human, bias_mouse, bias_human, counts, rows, columns)


def back_body(
    humans_ref, mouse_ref, human_ref, early_ref, late_ref, out_ref, total_ref,
    *, mouse_tiles, early_tiles, tracks, windows,
):
    step = pl.program_id(0)
    tile = mouse_ref.shape[0]
    is_mouse = step < mouse_tiles
    row = lax.broadcasted_iota(jnp.int32, (tile, 1), 0)

    @pl.when(step == 0)
    def _():
        total_ref[...] = jnp.zeros_like(total_ref)

    @pl.when(is_mouse & (humans_ref[0] < windows))
    def _():
        inside = step * tile + row < tracks[1]
        weight = jnp.where(inside, mouse_ref[...], BF16(0)).T
        total_ref[...] += jnp.dot(weight, early_ref[...], preferred_element_type=F32)

    def human(grads_ref):
        inside = (step - mouse_tiles) * tile + row < tracks[0]
        weight = jnp.where(inside, human_ref[...], BF16(0)).T
        total_ref[...] += jnp.dot(weight, grads_ref[...], preferred_element_type=F32)

    some = humans_ref[0] > 0

    @pl.when((step >= mouse_tiles) & (step < early_tiles) & some)
    def _():
        human(early_ref)

    @pl.when((step >= early_tiles) & some)
    def _():
        human(late_ref)

    @pl.when(step == pl.num_programs(0) - 1)
    def _():
        out_ref[...] = total_ref[...].T


def head_back(humans, windows, mouse, human, early, late):
    tokens = early.shape[1]
    width = human.shape[1]
    mouse_tiles = pl.cdiv(mouse.shape[0], TILE)
    early_tiles = early.shape[0] // TILE
    tiles = early_tiles + late.shape[0] // TILE
    return pl.pallas_call(
        functools.partial(
            back_body,
            mouse_tiles=mouse_tiles,
            early_tiles=early_tiles,
            tracks=(human.shape[0], mouse.shape[0]),
            windows=windows,
        ),
        grid_spec=pltpu.PrefetchScalarGridSpec(
            num_scalar_prefetch=1,
            grid=(tiles,),
            in_specs=[
                pl.BlockSpec((TILE, width), lambda j, *_: (jnp.minimum(j, mouse_tiles - 1), 0)),
                pl.BlockSpec((TILE, width), lambda j, *_: (jnp.maximum(j - mouse_tiles, 0), 0)),
                pl.BlockSpec((TILE, tokens), lambda j, *_: (jnp.minimum(j, early_tiles - 1), 0)),
                pl.BlockSpec((TILE, tokens), lambda j, *_: (jnp.maximum(j - early_tiles, 0), 0)),
            ],
            out_specs=pl.BlockSpec((tokens, width), lambda j, *_: (0, 0)),
            scratch_shapes=[pltpu.VMEM((width, tokens), F32)],
        ),
        out_shape=jax.ShapeDtypeStruct((tokens, width), F32),
        compiler_params=pltpu.CompilerParams(vmem_limit_bytes=58 * 2**20),
        cost_estimate=pl.CostEstimate(
            flops=2 * tiles * TILE * width * tokens,
            bytes_accessed=tiles * TILE * (tokens + width) * 2,
            transcendentals=0,
        ),
    )(humans, mouse, human, early, late)


def widen_body(in_ref, out_ref):
    out_ref[...] = in_ref[0].astype(F32)


def widen_head(tracks, summed, before, early):
    devices, rows, width = summed.shape
    block = rows // 2
    place = lambda j: (jnp.where(j < early, before + j, j - early), jnp.where(j < early, 0, 1), 0)
    return pl.pallas_call(
        widen_body,
        grid=(pl.cdiv(tracks, block),),
        in_specs=[pl.BlockSpec((1, block, width), place)],
        out_specs=pl.BlockSpec((block, width), lambda j: (j, 0)),
        out_shape=jax.ShapeDtypeStruct((tracks, width), F32),
        compiler_params=pltpu.CompilerParams(vmem_limit_bytes=60 * 2**20),
    )(summed)


def weights_body(core_ref, mine_ref, other_ref, conv_ref, proj_ref, sums_ref):
    half, middle = mine_ref.shape
    taken = conv_ref.shape[0]
    strips = proj_ref.shape[1] // middle

    def spread(first, second):
        def rows(start, count):
            parts = []
            if start < half:
                parts.append(first[start : min(half, start + count), :])
            if start + count > half:
                parts.append(second[max(0, start - half) : start + count - half, :])
            parts = [part.astype(F32) for part in parts]
            return parts[0] if len(parts) == 1 else jnp.concatenate(parts, axis=0)

        conv_ref[...] = rows(0, taken)
        for i in range(strips):
            proj_ref[:, i * middle : (i + 1) * middle] = rows(
                taken + i * proj_ref.shape[0], proj_ref.shape[0]
            )
        sums_ref[...] = rows(taken + strips * proj_ref.shape[0], sums_ref.shape[0])

    @pl.when(core_ref[0] == 0)
    def _():
        spread(mine_ref, other_ref)

    @pl.when(core_ref[0] != 0)
    def _():
        spread(other_ref, mine_ref)


def finish_weights(core, mine, other, taken, proj_shape):
    half, middle = mine.shape
    rest = 2 * half - taken - proj_shape[0] * proj_shape[1] // middle
    shapes = [(taken, middle), proj_shape, (rest, middle)]
    whole = lambda shape: pl.BlockSpec(shape, lambda j, *_: (0, 0))
    return pl.pallas_call(
        weights_body,
        grid_spec=pltpu.PrefetchScalarGridSpec(
            num_scalar_prefetch=1,
            grid=(1,),
            in_specs=[whole((half, middle))] * 2,
            out_specs=[whole(shape) for shape in shapes],
        ),
        out_shape=[jax.ShapeDtypeStruct(shape, F32) for shape in shapes],
        compiler_params=pltpu.CompilerParams(vmem_limit_bytes=60 * 2**20),
    )(core, mine, other)


def on_device(
    block_in,
    gain_in,
    shift_in,
    dilated_taps_weight,
    gain_mid,
    shift_mid,
    proj_weight,
    proj_bias,
    head_human,
    bias_human,
    head_mouse,
    bias_mouse,
    species,
    counts,
):
    windows, span, width = block_in.shape
    tokens = windows * span
    middle = proj_weight.shape[0]
    tracks_human = head_human.shape[1]
    tracks_mouse = head_mouse.shape[1]
    devices = lax.axis_size(EVERY)
    population = float(tokens * devices)
    core = lax.axis_index("core").astype(jnp.int32)[None]

    wide = block_in.reshape(tokens, width).astype(F32)
    sent, finish = small_sum([jnp.sum(wide, axis=0), jnp.sum(wide * wide, axis=0)])
    before, after = [move(value) for value, move in edges(block_in, DILATION_STEP)]
    everyone = to_all(sent)
    sum_in, square_in = finish(everyone)
    centre_in, scale_in = statistics(sum_in, square_in, population)

    def activate_in(values):
        return gelu_pair((values.astype(F32) - centre_in) * scale_in * gain_in + shift_in)

    normed_in = (wide - centre_in) * scale_in
    hidden_in, slope_in = gelu_pair(normed_in * gain_in + shift_in)
    hidden_in = hidden_in.astype(BF16).reshape(windows, span, width)
    place = lax.axis_index(BINS)
    last = lax.axis_size(BINS) - 1
    hidden_before = jnp.where(place > 0, activate_in(before)[0], 0.0).astype(BF16)
    hidden_after = jnp.where(place < last, activate_in(after)[0], 0.0).astype(BF16)
    padded = jnp.concatenate([hidden_before, hidden_in, hidden_after], axis=1)
    shifted = taps(padded, span)
    dilated = sum(
        jnp.dot(rows, dilated_taps_weight[k], preferred_element_type=F32)
        for k, rows in enumerate(shifted)
    )
    sent, finish = small_sum([jnp.sum(dilated, axis=0), jnp.sum(dilated * dilated, axis=0)])
    sum_mid, square_mid = finish(to_all(sent))
    centre_mid, scale_mid = statistics(sum_mid, square_mid, population)
    normed_mid = (dilated - centre_mid) * scale_mid
    hidden_mid, slope_mid = gelu_pair(normed_mid * gain_mid + shift_mid)
    hidden_mid = hidden_mid.astype(BF16)
    branch = jnp.dot(hidden_mid, proj_weight, preferred_element_type=F32)
    block_out = (wide + branch + proj_bias).astype(BF16)

    lane = min(span, LANES)
    counts_rows = (
        counts.transpose(2, 0, 1)
        .reshape(tracks_human, windows, span // lane, lane)
        .transpose(0, 2, 1, 3)
        .reshape(-1, lane)
    )
    columns = block_out.T
    scales = (math.sqrt(width / tracks_human), math.sqrt(width / tracks_mouse))
    by_species = jnp.argsort(species).astype(jnp.int32)
    humans = jnp.sum(species == 0).astype(jnp.int32)[None]
    mouse_tiles, human_tiles = pl.cdiv(tracks_mouse, TILE), pl.cdiv(tracks_human, TILE)
    early_tiles = (mouse_tiles + human_tiles) // 2 - mouse_tiles
    late_tiles = human_tiles - early_tiles
    mouse, human = head_mouse.T, head_human.T

    def some_tiles(*which):
        return head(
            species, by_species, humans, core, mouse, human, bias_mouse[None], bias_human[None],
            counts_rows, block_out, columns, scales, *which,
        )

    scatter = lambda value, axes: lax.psum_scatter(value, axes, scatter_dimension=0, tiled=True)
    gather = lambda value, axes: lax.all_gather(value, axes, axis=0, tiled=True)
    across, along, deep = bits_of("x"), bits_of("y"), bits_of("batch")
    order = Order()
    early, slopes_early, bias_early = some_tiles(mouse_tiles, 0, early_tiles, False)
    order.token = [bias_early]
    early = scatter(early, BINS)
    late, slopes_late, bias_late = order.run(
        lambda *_: some_tiles(0, early_tiles, late_tiles, False), bias_early
    )
    order.token = [bias_late]
    late = scatter(late, BINS)
    output_grad = order.run(
        lambda early, late: head_back(humans, windows, mouse, human, early, late),
        slopes_early,
        slopes_late,
    )
    to_core = lambda value: swap(value, CORE)
    chips = lax.axis_size(CHIPS)
    unit = 16 * chips

    def cut(rows, count):
        count = min(count, rows // unit)
        ends = [rows // unit * (i + 1) // count * unit for i in range(count)]
        return [end - start for end, start in zip(ends, [0] + ends[:-1])]

    def after_head(output_grad):
        branch_grad = output_grad.astype(BF16)
        mid_grad = back_product(branch_grad, proj_weight) * slope_mid
        sent, _ = small_sum([jnp.sum(mid_grad, axis=0), jnp.sum(mid_grad * normed_mid, axis=0)])
        return sent, branch_grad, mid_grad

    sent, branch_grad, mid_grad = order.run(after_head, output_grad)
    everyone = to_all(sent)

    def weight_work(branch_grad, output_grad):
        product = rows_product(hidden_mid, branch_grad).reshape(middle, width // middle, middle)
        return product.swapaxes(0, 1).reshape(-1, middle), jnp.sum(output_grad, axis=0)

    proj_grad, proj_bias_grad = order.run(weight_work, branch_grad, output_grad)

    def middle_work(everyone, mid_grad):
        _, finish = small_sum([shift_mid, gain_mid])
        shift_mid_grad, gain_mid_grad = finish(everyone)
        dilated_grad = scale_mid * gain_mid * (
            mid_grad - shift_mid_grad / population - normed_mid * gain_mid_grad / population
        )
        return dilated_grad.astype(BF16), shift_mid_grad, gain_mid_grad

    dilated_grad, shift_mid_grad, gain_mid_grad = order.run(middle_work, everyone, mid_grad)
    dilated_windows = dilated_grad.reshape(windows, span, middle)
    grad_before, grad_after = [move(value) for value, move in edges(dilated_windows, DILATION_STEP)]
    sums = jnp.concatenate(
        [
            proj_bias_grad,
            bias_early[0, mouse_tiles * TILE :],
            bias_late[0, : tracks_human - early_tiles * TILE],
            bias_early[0, :tracks_mouse],
        ]
    )
    weight_rows = pl.cdiv(4 * width * middle + sums.size, middle)
    all_rows = pl.cdiv(weight_rows, 4 * unit) * 4 * unit
    half = all_rows // 2

    def conv_work(dilated_grad, proj_grad, sums):
        parts = [rows_product(rows, dilated_grad) for rows in shifted] + [proj_grad]
        fill = (all_rows - 4 * width) * middle - sums.size
        parts.append(jnp.pad(sums, (0, fill)).reshape(-1, middle))
        grads = jnp.concatenate(parts, axis=0)
        return lax.dynamic_slice_in_dim(grads, (1 - core[0]) * half, half, 0), grads

    weights_send, weights_grad = order.run(conv_work, dilated_grad, proj_grad, sums)
    weights_arrived = to_core(weights_send)
    weights_keep = lax.dynamic_slice_in_dim(weights_grad, core[0] * half, half, 0)
    weights = Group(
        order,
        [weights_keep, weights_arrived],
        cut(half, 2),
        0,
        (across + along + deep, along + across + deep),
    )
    weights.step()

    def hidden_work(grad_before, dilated_windows, grad_after):
        grad_shifted = taps(
            jnp.concatenate([grad_before, dilated_windows, grad_after], axis=1), span
        )
        hidden_grad = sum(
            back_product(grad_shifted[2 - k], dilated_taps_weight[k]) for k in range(3)
        )
        in_grad = hidden_grad * slope_in
        sent, _ = small_sum([jnp.sum(in_grad, axis=0), jnp.sum(in_grad * normed_in, axis=0)])
        return sent, in_grad

    sent, in_grad = order.run(hidden_work, grad_before, dilated_windows, grad_after)
    everyone = to_all(sent)
    weights.step()

    def last_work(everyone, output_grad, in_grad):
        _, finish = small_sum([shift_in, gain_in])
        shift_in_grad, gain_in_grad = finish(everyone)
        input_grad = output_grad + scale_in * gain_in * (
            in_grad - shift_in_grad / population - normed_in * gain_in_grad / population
        )
        return input_grad.astype(BF16), shift_in_grad, gain_in_grad

    input_grad, shift_in_grad, gain_in_grad = order.run(last_work, everyone, output_grad, in_grad)
    weights.step()
    summed = order.run(lambda *both: jnp.concatenate(both, axis=0), early, late)
    summed = scatter(summed, "batch")
    weights.step()
    weights.step()
    summed = gather(order.run(lambda value: value, summed), "batch")
    weights.step()
    weights.step()
    summed = gather(order.run(lambda value: value, summed), BINS)
    while not weights.done():
        weights.step()
    summed = summed.reshape(lax.axis_size(BINS), -1, width)
    weights_mine = weights.shares[0]
    weights_other = to_core(weights_mine)
    conv_total, proj_total, sums_total = order.run(
        lambda mine, other: finish_weights(core, mine, other, 3 * width, (middle, width)),
        weights_mine,
        weights_other,
    )
    conv_total = conv_total.reshape(3, width, middle)
    conv_total = conv_total.reshape(3, width, middle)
    sums_total = sums_total.reshape(-1)
    ends = [0, width, width + tracks_human, width + tracks_human + tracks_mouse]
    proj_bias_total, bias_human_grad, bias_mouse_grad = [
        sums_total[low:high] for low, high in zip(ends[:-1], ends[1:])
    ]
    per_tile = TILE // (summed.shape[1] // 2)
    mouse_blocks, early_blocks = mouse_tiles * per_tile, early_tiles * per_tile
    head_mouse_grad = widen_head(tracks_mouse, summed, 0, mouse_blocks)
    head_human_grad = widen_head(tracks_human, summed, mouse_blocks, early_blocks)
    return (
        block_out.reshape(windows, span, width),
        input_grad.reshape(windows, span, width),
        gain_in_grad,
        shift_in_grad,
        conv_total,
        gain_mid_grad,
        shift_mid_grad,
        proj_total,
        proj_bias_total,
        head_human_grad.T,
        bias_human_grad,
        head_mouse_grad.T,
        bias_mouse_grad,
    )


def solution(mesh):
    bins, batch = mesh.shape["bins"], mesh.shape["batch"]
    side = 1 << (((bins // 2).bit_length() - 1) // 2)
    grid = jax.sharding.Mesh(
        mesh.devices.reshape(bins // 2 // side, side, 2, batch), ("y", "x", "core", "batch")
    )
    tokens = P("batch", BINS, None)
    placed = (tokens,) + (P(),) * 11 + (P("batch"), tokens)
    return jax.shard_map(
        on_device,
        mesh=grid,
        in_specs=placed,
        out_specs=(tokens, tokens) + (P(),) * 11,
        check_vma=False,
    )
```

```python
import functools
import math

import jax
import jax.numpy as jnp
from jax import lax
from jax.experimental import pallas as pl
from jax.experimental.pallas import tpu as pltpu
from jax.sharding import PartitionSpec as P

DILATION_STEP = 11
EPS = 1e-05
F32 = jnp.float32
BF16 = jnp.bfloat16
EVERY = ("y", "x", "core", "batch")
BINS = ("y", "x", "core")
CHIPS = ("y", "x", "batch")
CORE = ("core", 1)
LANES = 128
TILE = 896


def bits_of(axis):
    return [(axis, 1 << i) for i in range(lax.axis_size(axis).bit_length() - 1)]


def small_sum(parts):
    flat = jnp.concatenate([part.reshape(-1) for part in parts])
    peers = lax.axis_size(EVERY)
    sent = jnp.broadcast_to(flat[None], (peers, flat.shape[0]))
    cuts = [part.size for part in parts]

    def finish(everyone):
        total = jnp.sum(everyone, axis=0)
        ends = [sum(cuts[: i + 1]) for i in range(len(cuts))]
        return [
            total[end - cut : end].reshape(part.shape)
            for part, cut, end in zip(parts, cuts, ends)
        ]

    return sent, finish


def to_all(sent, axes=EVERY):
    return lax.all_to_all(sent, axes, 0, 0, tiled=True)


def swap(value, stage):
    axis, mask = stage
    size = lax.axis_size(axis)
    return lax.ppermute(value, axis, [(i, i ^ mask) for i in range(size)])


def upper(stage):
    axis, mask = stage
    return ((lax.axis_index(axis) & mask) != 0).astype(jnp.int32)


def sum_body(at_ref, *refs, counts):
    ins, outs = refs[: sum(counts)], refs[sum(counts) :]
    used = 0
    for out, count in zip(outs, counts):
        total = sum(ref[...].astype(F32) for ref in ins[used : used + count])
        out[...] = total.astype(out.dtype)
        used += count


def sum_parts(parts, dtype):
    if any(rows % 16 for rows, _ in parts):
        sums = [
            sum(lax.dynamic_slice_in_dim(a, at, rows, 0).astype(F32) for a, at in pieces)
            for rows, pieces in parts
        ]
        return [value.astype(dtype) for value in sums]
    lanes = parts[0][1][0][0].shape[1]
    places, specs, values, counts, shapes = [], [], [], [], []
    for rows, pieces in parts:
        for array, at in pieces:
            specs.append(
                pl.BlockSpec((rows, lanes), lambda j, at_ref, i=len(places): (at_ref[i], 0))
            )
            places.append(jnp.asarray(at, jnp.int32) // rows)
            values.append(array)
        counts.append(len(pieces))
        shapes.append(rows)
    return pl.pallas_call(
        functools.partial(sum_body, counts=counts),
        grid_spec=pltpu.PrefetchScalarGridSpec(
            num_scalar_prefetch=1,
            grid=(1,),
            in_specs=specs,
            out_specs=[pl.BlockSpec((rows, lanes), lambda j, *_: (0, 0)) for rows in shapes],
        ),
        out_shape=[jax.ShapeDtypeStruct((rows, lanes), dtype) for rows in shapes],
        compiler_params=pltpu.CompilerParams(vmem_limit_bytes=60 * 2**20),
    )(jnp.stack(places), *values)


def join_body(mine_ref, *refs, count, stacked):
    row = 0
    for i in range(count):
        share, arrived = refs[2 * i], refs[2 * i + 1]
        out = refs[2 * count + (0 if stacked else i)]
        rows = share.shape[0]
        mine = mine_ref[i]
        out[pl.ds(pl.multiple_of(row + mine * rows, 16), rows), :] = share[...]
        out[pl.ds(pl.multiple_of(row + (1 - mine) * rows, 16), rows), :] = arrived[...]
        if stacked:
            row += 2 * rows


def join_parts(parts, stacked=False):
    if any(share.shape[0] % 16 for share, _, _ in parts):
        joined = [
            jnp.concatenate([jnp.where(mine == 1, b, a), jnp.where(mine == 1, a, b)], axis=0)
            for a, b, mine in parts
        ]
        return [jnp.concatenate(joined, axis=0)] if stacked else joined
    outs = [2 * a.shape[0] for a, _, _ in parts]
    if stacked:
        outs = [sum(outs)]
    lanes = parts[0][0].shape[1]
    whole = lambda rows: pl.BlockSpec((rows, lanes), lambda j, *_: (0, 0))
    return pl.pallas_call(
        functools.partial(join_body, count=len(parts), stacked=stacked),
        grid_spec=pltpu.PrefetchScalarGridSpec(
            num_scalar_prefetch=1,
            grid=(1,),
            in_specs=[whole(v.shape[0]) for a, b, _ in parts for v in (a, b)],
            out_specs=[whole(rows) for rows in outs],
        ),
        out_shape=[jax.ShapeDtypeStruct((rows, lanes), BF16) for rows in outs],
        compiler_params=pltpu.CompilerParams(vmem_limit_bytes=60 * 2**20),
    )(jnp.stack([mine for _, _, mine in parts]), *[v for a, b, _ in parts for v in (a, b)])


class Group:
    def __init__(self, pieces, rows, routes):
        self.parts = [
            {"pieces": [(piece, at) for piece in pieces], "rows": count, "route": route}
            for at, count, route in zip(
                [sum(rows[:i]) for i in range(len(rows))], rows, routes
            )
        ]
        self.levels = len(routes[0])
        self.level = 0
        self.flying = None
        self.shares = None

    def work(self, arrays, flying):
        level = self.level
        if level > self.levels:
            back = 2 * self.levels - level
            return join_parts(
                [
                    (share, arrived, upper(part["route"][back]))
                    for share, arrived, part in zip(self.shares, flying, self.parts)
                ],
                stacked=level == 2 * self.levels,
            )
        wanted = []
        for i, part in enumerate(self.parts):
            pieces = list(zip(arrays[i], [at for _, at in part["pieces"]]))
            if level:
                mine = upper(part["route"][level - 1])
                pieces = [(a, at + mine * part["rows"]) for a, at in pieces]
                pieces.append((flying[i], 0))
            part["pieces"] = pieces
            if level < self.levels:
                part["rows"] //= 2
                away = 1 - upper(part["route"][level])
                pieces = [(a, at + away * part["rows"]) for a, at in pieces]
            wanted.append((part["rows"], pieces))
        return sum_parts(wanted, F32 if level < self.levels else BF16)

    def step(self, held=()):
        arrays = [[a for a, _ in part["pieces"]] for part in self.parts]
        values = self.work(arrays, self.flying)
        values, held = tie(values, held)
        if self.level >= self.levels:
            self.shares = values
        if self.level < 2 * self.levels:
            next_level = min(self.level, 2 * self.levels - 1 - self.level)
            self.flying = [
                swap(value, part["route"][next_level]) for value, part in zip(values, self.parts)
            ]
        self.level += 1
        return held

    def done(self):
        return self.level > 2 * self.levels


def tie(*values):
    return lax.optimization_barrier(values)


def gelu_pair(values):
    logistic = jax.nn.sigmoid(1.702 * values)
    return (values * logistic, logistic + 1.702 * values * logistic * (1.0 - logistic))


def rows_product(former, latter):
    return lax.dot_general(
        former, latter, (((0,), (0,)), ((), ())), preferred_element_type=F32
    )


def back_product(former, latter):
    return lax.dot_general(
        former, latter, (((1,), (1,)), ((), ())), preferred_element_type=F32
    )


def taps(padded_rows, span):
    windows = padded_rows.shape[0]
    return [
        padded_rows[:, k * DILATION_STEP : k * DILATION_STEP + span, :].reshape(
            windows * span, -1
        )
        for k in range(3)
    ]


def statistics(plain_sum, square_sum, population):
    centre = plain_sum / population
    return (centre, lax.rsqrt(square_sum / population - centre * centre + EPS))


def edges(shard, width):
    peers, length = (lax.axis_size(BINS), shard.shape[1])
    up = [(i, i + 1) for i in range(peers - 1)]
    down = [(i + 1, i) for i in range(peers - 1)]
    return (
        (shard[:, length - width :], lambda value: lax.ppermute(value, BINS, up)),
        (shard[:, :width], lambda value: lax.ppermute(value, BINS, down)),
    )


def poisson_slope(logits, counted):
    held = jnp.maximum(logits, -80.0)
    small = jnp.exp(-jnp.abs(held))
    whole = 1.0 + small
    tail = jnp.where(small < 1e-3, small * (1.0 - 0.5 * small), jnp.log(whole))
    rate = jnp.maximum(held, 0.0) + tail
    top = jnp.where(held >= 0.0, 1.0, small)
    return top * (rate - counted) / (whole * rate)


def head_body(
    species_ref,
    windows_ref,
    humans_ref,
    mouse_ref,
    human_ref,
    bias_mouse_ref,
    bias_human_ref,
    counts_ref,
    rows_ref,
    columns_ref,
    out_ref,
    grads_ref,
    bias_grad_ref,
    weight_ref,
    bias_ref,
    sums_ref,
    *,
    mouse_tiles,
    tracks,
    scales,
):
    step = pl.program_id(0)
    tile, width = weight_ref.shape
    windows = windows_ref.shape[0]
    span = rows_ref.shape[0] // windows
    lane = counts_ref.shape[1]
    groups = span // lane
    is_mouse = step < mouse_tiles
    humans = humans_ref[0]
    active = jnp.where(is_mouse, windows - humans, humans)
    skipped = jnp.where(is_mouse, humans, 0)
    first = jnp.where(is_mouse, step, step - mouse_tiles) * tile
    end = jnp.where(is_mouse, tracks[1], tracks[0])
    scale = jnp.where(is_mouse, scales[1], scales[0]).astype(F32)

    def prepare():
        inside = first + lax.broadcasted_iota(jnp.int32, (tile, 1), 0) < end

        @pl.when(is_mouse)
        def _():
            weight_ref[...] = jnp.where(inside, mouse_ref[...], BF16(0))
            bias_ref[...] = jnp.broadcast_to(bias_mouse_ref[...], (LANES, tile)).T

        @pl.when(jnp.logical_not(is_mouse))
        def _():
            weight_ref[...] = jnp.where(inside, human_ref[...], BF16(0))
            bias_ref[...] = jnp.broadcast_to(bias_human_ref[...], (LANES, tile)).T

    def slopes(logits, window, scale):
        inside = first + lax.broadcasted_iota(jnp.int32, (tile, 1), 0) < end
        total = jnp.zeros((tile, lane), F32)
        low = []
        for h in range(groups):
            counted = counts_ref[
                pl.ds(h * windows + window, tile, stride=groups * windows), :
            ].astype(F32)
            part = logits[:, h * lane : (h + 1) * lane] + bias_ref[:, :lane]
            slope = jnp.where(inside, poisson_slope(part, counted) * scale, 0.0)
            total = total + slope
            low.append(slope.astype(BF16))
        return total, jnp.concatenate(low, axis=1)

    @pl.when(active == 0)
    def _():
        out_ref[...] = jnp.zeros_like(out_ref)
        grads_ref[...] = jnp.zeros_like(grads_ref)
        bias_grad_ref[...] = jnp.zeros_like(bias_grad_ref)

    @pl.when(active * 4 >= windows * 3)
    def _():
        prepare()
        total = None
        for i in range(windows):
            lanes = slice(i * span, (i + 1) * span)
            logits = jnp.dot(weight_ref[...], columns_ref[:, lanes], preferred_element_type=F32)
            part, low = slopes(
                logits, i, jnp.where((species_ref[i] == 1) == is_mouse, scale, 0.0)
            )
            total = part if total is None else total + part
            grads_ref[:, lanes] = low
        bias_grad_ref[...] = jnp.sum(total.T, axis=0, keepdims=True)
        product = jnp.dot(grads_ref[...], rows_ref[...], preferred_element_type=F32)
        out_ref[...] = product.astype(BF16)

    @pl.when((active > 0) & (active * 4 < windows * 3))
    def _():
        prepare()
        grads_ref[...] = jnp.zeros_like(grads_ref)
        sums_ref[...] = jnp.zeros_like(sums_ref)

        def one(window):
            at = window * span
            lanes = pl.ds(at if isinstance(window, int) else pl.multiple_of(at, span), span)
            logits = jnp.dot(weight_ref[...], columns_ref[:, lanes], preferred_element_type=F32)
            part, low = slopes(logits, window, scale)
            sums_ref[...] += part
            grads_ref[:, lanes] = low
            return 0

        if span % LANES == 0:
            lax.fori_loop(0, active, lambda i, _: one(windows_ref[skipped + i]), 0)
        else:
            for i in range(windows):

                @pl.when((species_ref[i] == 1) == is_mouse)
                def _():
                    one(i)
        bias_grad_ref[...] = jnp.sum(sums_ref[...].T, axis=0, keepdims=True)
        product = jnp.dot(grads_ref[...], rows_ref[...], preferred_element_type=F32)
        out_ref[...] = product.astype(BF16)


def head(
    species, order, humans, mouse, human, bias_mouse, bias_human, counts, rows, columns, scales
):
    tokens, width = rows.shape
    lane = counts.shape[1]
    tracks = (human.shape[0], mouse.shape[0])
    mouse_tiles = pl.cdiv(tracks[1], TILE)
    tiles = mouse_tiles + pl.cdiv(tracks[0], TILE)
    at_mouse = lambda j: jnp.minimum(j, mouse_tiles - 1)
    at_human = lambda j: jnp.maximum(j - mouse_tiles, 0)
    at_both = lambda j: jnp.where(j < mouse_tiles, j, j - mouse_tiles)
    fixed = lambda j, *_: (0, 0)
    out = lambda j, *_: (j, 0)
    return pl.pallas_call(
        functools.partial(head_body, mouse_tiles=mouse_tiles, tracks=tracks, scales=scales),
        grid_spec=pltpu.PrefetchScalarGridSpec(
            num_scalar_prefetch=3,
            grid=(tiles,),
            in_specs=[
                pl.BlockSpec((TILE, width), lambda j, *_: (at_mouse(j), 0)),
                pl.BlockSpec((TILE, width), lambda j, *_: (at_human(j), 0)),
                pl.BlockSpec((1, TILE), lambda j, *_: (0, at_mouse(j))),
                pl.BlockSpec((1, TILE), lambda j, *_: (0, at_human(j))),
                pl.BlockSpec((TILE * tokens // lane, lane), lambda j, *_: (at_both(j), 0)),
                pl.BlockSpec((tokens, width), fixed),
                pl.BlockSpec((width, tokens), fixed),
            ],
            out_specs=[
                pl.BlockSpec((TILE, width), out),
                pl.BlockSpec((TILE, tokens), out),
                pl.BlockSpec((1, TILE), lambda j, *_: (0, j)),
            ],
            scratch_shapes=[
                pltpu.VMEM((TILE, width), BF16),
                pltpu.VMEM((TILE, LANES), F32),
                pltpu.VMEM((TILE, lane), F32),
            ],
        ),
        out_shape=[
            jax.ShapeDtypeStruct((tiles * TILE, width), BF16),
            jax.ShapeDtypeStruct((tiles * TILE, tokens), BF16),
            jax.ShapeDtypeStruct((1, tiles * TILE), F32),
        ],
        compiler_params=pltpu.CompilerParams(vmem_limit_bytes=58 * 2**20),
        cost_estimate=pl.CostEstimate(
            flops=4 * tiles * TILE * width * tokens,
            bytes_accessed=tiles * TILE * (tokens * 6 + width * 4),
            transcendentals=3 * tiles * TILE * tokens,
        ),
    )(species, order, humans, mouse, human, bias_mouse, bias_human, counts, rows, columns)


def back_body(
    humans_ref, mouse_ref, human_ref, grads_ref, out_ref, total_ref, *, mouse_tiles, tracks, windows
):
    step = pl.program_id(0)
    tile = mouse_ref.shape[0]
    is_mouse = step < mouse_tiles
    row = lax.broadcasted_iota(jnp.int32, (tile, 1), 0)

    @pl.when(step == 0)
    def _():
        total_ref[...] = jnp.zeros_like(total_ref)

    @pl.when(is_mouse & (humans_ref[0] < windows))
    def _():
        inside = step * tile + row < tracks[1]
        weight = jnp.where(inside, mouse_ref[...], BF16(0)).T
        total_ref[...] += jnp.dot(weight, grads_ref[...], preferred_element_type=F32)

    @pl.when((step >= mouse_tiles) & (humans_ref[0] > 0))
    def _():
        inside = (step - mouse_tiles) * tile + row < tracks[0]
        weight = jnp.where(inside, human_ref[...], BF16(0)).T
        total_ref[...] += jnp.dot(weight, grads_ref[...], preferred_element_type=F32)

    @pl.when(step == pl.num_programs(0) - 1)
    def _():
        out_ref[...] = total_ref[...].T


def head_back(humans, windows, mouse, human, grads):
    tokens = grads.shape[1]
    width = human.shape[1]
    mouse_tiles = pl.cdiv(mouse.shape[0], TILE)
    tiles = grads.shape[0] // TILE
    return pl.pallas_call(
        functools.partial(
            back_body,
            mouse_tiles=mouse_tiles,
            tracks=(human.shape[0], mouse.shape[0]),
            windows=windows,
        ),
        grid_spec=pltpu.PrefetchScalarGridSpec(
            num_scalar_prefetch=1,
            grid=(tiles,),
            in_specs=[
                pl.BlockSpec((TILE, width), lambda j, *_: (jnp.minimum(j, mouse_tiles - 1), 0)),
                pl.BlockSpec((TILE, width), lambda j, *_: (jnp.maximum(j - mouse_tiles, 0), 0)),
                pl.BlockSpec((TILE, tokens), lambda j, *_: (j, 0)),
            ],
            out_specs=pl.BlockSpec((tokens, width), lambda j, *_: (0, 0)),
            scratch_shapes=[pltpu.VMEM((width, tokens), F32)],
        ),
        out_shape=jax.ShapeDtypeStruct((tokens, width), F32),
        compiler_params=pltpu.CompilerParams(vmem_limit_bytes=58 * 2**20),
        cost_estimate=pl.CostEstimate(
            flops=2 * tiles * TILE * width * tokens,
            bytes_accessed=tiles * TILE * (tokens + width) * 2,
            transcendentals=0,
        ),
    )(humans, mouse, human, grads)


def widen_body(in_ref, out_ref):
    out_ref[...] = in_ref[0].astype(F32)


def widen_head(tracks, summed, first):
    _, block, width = summed.shape
    return pl.pallas_call(
        widen_body,
        grid=(pl.cdiv(tracks, block),),
        in_specs=[pl.BlockSpec((1, block, width), lambda j: (first // block + j, 0, 0))],
        out_specs=pl.BlockSpec((block, width), lambda j: (j, 0)),
        out_shape=jax.ShapeDtypeStruct((tracks, width), F32),
        compiler_params=pltpu.CompilerParams(vmem_limit_bytes=60 * 2**20),
    )(summed)


def weights_body(core_ref, mine_ref, other_ref, conv_ref, proj_ref, sums_ref):
    half, middle = mine_ref.shape
    taken = conv_ref.shape[0]
    strips = proj_ref.shape[1] // middle

    def spread(first, second):
        def rows(start, count):
            parts = []
            if start < half:
                parts.append(first[start : min(half, start + count), :])
            if start + count > half:
                parts.append(second[max(0, start - half) : start + count - half, :])
            parts = [part.astype(F32) for part in parts]
            return parts[0] if len(parts) == 1 else jnp.concatenate(parts, axis=0)

        conv_ref[...] = rows(0, taken)
        for i in range(strips):
            proj_ref[:, i * middle : (i + 1) * middle] = rows(
                taken + i * proj_ref.shape[0], proj_ref.shape[0]
            )
        sums_ref[...] = rows(taken + strips * proj_ref.shape[0], sums_ref.shape[0])

    @pl.when(core_ref[0] == 0)
    def _():
        spread(mine_ref, other_ref)

    @pl.when(core_ref[0] != 0)
    def _():
        spread(other_ref, mine_ref)


def finish_weights(core, mine, other, taken, proj_shape):
    half, middle = mine.shape
    rest = 2 * half - taken - proj_shape[0] * proj_shape[1] // middle
    shapes = [(taken, middle), proj_shape, (rest, middle)]
    whole = lambda shape: pl.BlockSpec(shape, lambda j, *_: (0, 0))
    return pl.pallas_call(
        weights_body,
        grid_spec=pltpu.PrefetchScalarGridSpec(
            num_scalar_prefetch=1,
            grid=(1,),
            in_specs=[whole((half, middle))] * 2,
            out_specs=[whole(shape) for shape in shapes],
        ),
        out_shape=[jax.ShapeDtypeStruct(shape, F32) for shape in shapes],
        compiler_params=pltpu.CompilerParams(vmem_limit_bytes=60 * 2**20),
    )(core, mine, other)


def on_device(
    block_in,
    gain_in,
    shift_in,
    dilated_taps_weight,
    gain_mid,
    shift_mid,
    proj_weight,
    proj_bias,
    head_human,
    bias_human,
    head_mouse,
    bias_mouse,
    species,
    counts,
):
    windows, span, width = block_in.shape
    tokens = windows * span
    middle = proj_weight.shape[0]
    tracks_human = head_human.shape[1]
    tracks_mouse = head_mouse.shape[1]
    devices = lax.axis_size(EVERY)
    population = float(tokens * devices)
    core = lax.axis_index("core").astype(jnp.int32)[None]

    wide = block_in.reshape(tokens, width).astype(F32)
    sent, finish = small_sum([jnp.sum(wide, axis=0), jnp.sum(wide * wide, axis=0)])
    before, after = [move(value) for value, move in edges(block_in, DILATION_STEP)]
    everyone = to_all(sent)
    sum_in, square_in = finish(everyone)
    centre_in, scale_in = statistics(sum_in, square_in, population)

    def activate_in(values):
        return gelu_pair((values.astype(F32) - centre_in) * scale_in * gain_in + shift_in)

    normed_in = (wide - centre_in) * scale_in
    hidden_in, slope_in = gelu_pair(normed_in * gain_in + shift_in)
    hidden_in = hidden_in.astype(BF16).reshape(windows, span, width)
    place = lax.axis_index(BINS)
    last = lax.axis_size(BINS) - 1
    hidden_before = jnp.where(place > 0, activate_in(before)[0], 0.0).astype(BF16)
    hidden_after = jnp.where(place < last, activate_in(after)[0], 0.0).astype(BF16)
    padded = jnp.concatenate([hidden_before, hidden_in, hidden_after], axis=1)
    shifted = taps(padded, span)
    dilated = sum(
        jnp.dot(rows, dilated_taps_weight[k], preferred_element_type=F32)
        for k, rows in enumerate(shifted)
    )
    sent, finish = small_sum([jnp.sum(dilated, axis=0), jnp.sum(dilated * dilated, axis=0)])
    sum_mid, square_mid = finish(to_all(sent))
    centre_mid, scale_mid = statistics(sum_mid, square_mid, population)
    normed_mid = (dilated - centre_mid) * scale_mid
    hidden_mid, slope_mid = gelu_pair(normed_mid * gain_mid + shift_mid)
    hidden_mid = hidden_mid.astype(BF16)
    branch = jnp.dot(hidden_mid, proj_weight, preferred_element_type=F32)
    block_out = (wide + branch + proj_bias).astype(BF16)

    lane = min(span, LANES)
    counts_rows = (
        counts.transpose(2, 0, 1)
        .reshape(tracks_human, windows, span // lane, lane)
        .transpose(0, 2, 1, 3)
        .reshape(-1, lane)
    )
    columns = block_out.T
    scales = (math.sqrt(width / tracks_human), math.sqrt(width / tracks_mouse))
    by_species = jnp.argsort(species).astype(jnp.int32)
    humans = jnp.sum(species == 0).astype(jnp.int32)[None]
    mouse_tiles, human_tiles = pl.cdiv(tracks_mouse, TILE), pl.cdiv(tracks_human, TILE)
    mouse, human = head_mouse.T, head_human.T

    scatter = lambda value, axes: lax.psum_scatter(value, axes, scatter_dimension=0, tiled=True)
    gather = lambda value, axes: lax.all_gather(value, axes)
    across, along, deep = bits_of("x"), bits_of("y"), bits_of("batch")
    grads, slopes, bias_grads = head(
        species, by_species, humans, mouse, human, bias_mouse[None], bias_human[None],
        counts_rows, block_out, columns, scales,
    )
    summed = scatter(grads, BINS)
    output_grad = head_back(humans, windows, mouse, human, slopes)
    to_core = lambda value: swap(value, CORE)
    chips = lax.axis_size(CHIPS)
    unit = 16 * chips

    def after_head(output_grad):
        branch_grad = output_grad.astype(BF16)
        mid_grad = back_product(branch_grad, proj_weight) * slope_mid
        sent, _ = small_sum([jnp.sum(mid_grad, axis=0), jnp.sum(mid_grad * normed_mid, axis=0)])
        return sent, branch_grad, mid_grad

    sent, branch_grad, mid_grad = after_head(output_grad)
    everyone = to_all(sent)

    def weight_work(branch_grad, output_grad):
        product = rows_product(hidden_mid, branch_grad).reshape(middle, width // middle, middle)
        return product.swapaxes(0, 1).reshape(-1, middle), jnp.sum(output_grad, axis=0)

    proj_grad, proj_bias_grad = weight_work(branch_grad, output_grad)

    def middle_work(everyone, mid_grad):
        _, finish = small_sum([shift_mid, gain_mid])
        shift_mid_grad, gain_mid_grad = finish(everyone)
        dilated_grad = scale_mid * gain_mid * (
            mid_grad - shift_mid_grad / population - normed_mid * gain_mid_grad / population
        )
        return dilated_grad.astype(BF16), shift_mid_grad, gain_mid_grad

    dilated_grad, shift_mid_grad, gain_mid_grad = middle_work(everyone, mid_grad)
    dilated_windows = dilated_grad.reshape(windows, span, middle)
    grad_before, grad_after = [move(value) for value, move in edges(dilated_windows, DILATION_STEP)]
    sums = jnp.concatenate(
        [
            proj_bias_grad,
            bias_grads[0, mouse_tiles * TILE : mouse_tiles * TILE + tracks_human],
            bias_grads[0, :tracks_mouse],
        ]
    )
    weight_rows = pl.cdiv(4 * width * middle + sums.size, middle)
    all_rows = pl.cdiv(weight_rows, 4 * unit) * 4 * unit
    half = all_rows // 2

    def conv_work(dilated_grad, proj_grad, sums):
        parts = [rows_product(rows, dilated_grad) for rows in shifted] + [proj_grad]
        fill = (all_rows - 4 * width) * middle - sums.size
        parts.append(jnp.pad(sums, (0, fill)).reshape(-1, middle))
        grads = jnp.concatenate(parts, axis=0)
        return lax.dynamic_slice_in_dim(grads, (1 - core[0]) * half, half, 0), grads

    weights_send, weights_grad = conv_work(dilated_grad, proj_grad, sums)
    weights_arrived = to_core(weights_send)
    weights_keep = lax.dynamic_slice_in_dim(weights_grad, core[0] * half, half, 0)
    weights = Group(
        [weights_keep, weights_arrived],
        [half // 2] * 2,
        (across + along + deep, along + across + deep),
    )
    grad_before = weights.step(grad_before)

    def hidden_work(grad_before, dilated_windows, grad_after):
        grad_shifted = taps(
            jnp.concatenate([grad_before, dilated_windows, grad_after], axis=1), span
        )
        hidden_grad = sum(
            back_product(grad_shifted[2 - k], dilated_taps_weight[k]) for k in range(3)
        )
        in_grad = hidden_grad * slope_in
        sent, _ = small_sum([jnp.sum(in_grad, axis=0), jnp.sum(in_grad * normed_in, axis=0)])
        return sent, in_grad

    sent, in_grad = hidden_work(grad_before, dilated_windows, grad_after)
    everyone = to_all(sent)
    summed, in_grad = tie(summed, in_grad)
    summed = scatter(summed, "batch")
    weights.step()
    everyone = weights.step(everyone)
    summed = weights.step(summed)
    summed = gather(summed, "batch").reshape(-1, width)
    summed = weights.step(summed)
    summed = gather(summed, BINS)

    def last_work(everyone, output_grad, in_grad):
        _, finish = small_sum([shift_in, gain_in])
        shift_in_grad, gain_in_grad = finish(everyone)
        input_grad = output_grad + scale_in * gain_in * (
            in_grad - shift_in_grad / population - normed_in * gain_in_grad / population
        )
        return input_grad.astype(BF16), shift_in_grad, gain_in_grad

    input_grad, shift_in_grad, gain_in_grad = last_work(everyone, output_grad, in_grad)
    while not weights.done():
        weights.step()
    weights_mine = weights.shares[0]
    conv_total, proj_total, sums_total = finish_weights(
        core, weights_mine, to_core(weights_mine), 3 * width, (middle, width)
    )
    conv_total = conv_total.reshape(3, width, middle)
    sums_total = sums_total.reshape(-1)
    ends = [0, width, width + tracks_human, width + tracks_human + tracks_mouse]
    proj_bias_total, bias_human_grad, bias_mouse_grad = [
        sums_total[low:high] for low, high in zip(ends[:-1], ends[1:])
    ]
    head_mouse_grad = widen_head(tracks_mouse, summed, 0)
    head_human_grad = widen_head(tracks_human, summed, mouse_tiles * TILE)
    return (
        block_out.reshape(windows, span, width),
        input_grad.reshape(windows, span, width),
        gain_in_grad,
        shift_in_grad,
        conv_total,
        gain_mid_grad,
        shift_mid_grad,
        proj_total,
        proj_bias_total,
        head_human_grad.T,
        bias_human_grad,
        head_mouse_grad.T,
        bias_mouse_grad,
    )


def solution(mesh):
    bins, batch = mesh.shape["bins"], mesh.shape["batch"]
    side = 1 << (((bins // 2).bit_length() - 1) // 2)
    grid = jax.sharding.Mesh(
        mesh.devices.reshape(bins // 2 // side, side, 2, batch), ("y", "x", "core", "batch")
    )
    tokens = P("batch", BINS, None)
    placed = (tokens,) + (P(),) * 11 + (P("batch"), tokens)
    return jax.shard_map(
        on_device,
        mesh=grid,
        in_specs=placed,
        out_specs=(tokens, tokens) + (P(),) * 11,
        check_vma=False,
    )
```

```python
import functools
import math

import jax
import jax.numpy as jnp
from jax import lax
from jax.experimental import pallas as pl
from jax.experimental.pallas import tpu as pltpu
from jax.sharding import PartitionSpec as P

DILATION_STEP = 11
EPS = 1e-05
F32 = jnp.float32
BF16 = jnp.bfloat16
EVERY = ("y", "x", "core", "batch")
BINS = ("y", "x", "core")
CHIPS = ("y", "x", "batch")
CORE = ("core", 1)
LANES = 128
TILE = 896


def bits_of(axis):
    return [(axis, 1 << i) for i in range(lax.axis_size(axis).bit_length() - 1)]


def small_sum(parts):
    flat = jnp.concatenate([part.reshape(-1) for part in parts])
    peers = lax.axis_size(EVERY)
    sent = jnp.broadcast_to(flat[None], (peers, flat.shape[0]))
    cuts = [part.size for part in parts]

    def finish(everyone):
        total = jnp.sum(everyone, axis=0)
        ends = [sum(cuts[: i + 1]) for i in range(len(cuts))]
        return [
            total[end - cut : end].reshape(part.shape)
            for part, cut, end in zip(parts, cuts, ends)
        ]

    return sent, finish


def to_all(sent, axes=EVERY):
    return lax.all_to_all(sent, axes, 0, 0, tiled=True)


def swap(value, stage):
    axis, mask = stage
    size = lax.axis_size(axis)
    return lax.ppermute(value, axis, [(i, i ^ mask) for i in range(size)])


def upper(stage):
    axis, mask = stage
    return ((lax.axis_index(axis) & mask) != 0).astype(jnp.int32)


def sum_body(at_ref, *refs, counts):
    ins, outs = refs[: sum(counts)], refs[sum(counts) :]
    used = 0
    for out, count in zip(outs, counts):
        total = sum(ref[...].astype(F32) for ref in ins[used : used + count])
        out[...] = total.astype(out.dtype)
        used += count


def sum_parts(parts, dtype):
    if any(rows % 16 for rows, _ in parts):
        sums = [
            sum(lax.dynamic_slice_in_dim(a, at, rows, 0).astype(F32) for a, at in pieces)
            for rows, pieces in parts
        ]
        return [value.astype(dtype) for value in sums]
    lanes = parts[0][1][0][0].shape[1]
    places, specs, values, counts, shapes = [], [], [], [], []
    for rows, pieces in parts:
        for array, at in pieces:
            specs.append(
                pl.BlockSpec((rows, lanes), lambda j, at_ref, i=len(places): (at_ref[i], 0))
            )
            places.append(jnp.asarray(at, jnp.int32) // rows)
            values.append(array)
        counts.append(len(pieces))
        shapes.append(rows)
    return pl.pallas_call(
        functools.partial(sum_body, counts=counts),
        grid_spec=pltpu.PrefetchScalarGridSpec(
            num_scalar_prefetch=1,
            grid=(1,),
            in_specs=specs,
            out_specs=[pl.BlockSpec((rows, lanes), lambda j, *_: (0, 0)) for rows in shapes],
        ),
        out_shape=[jax.ShapeDtypeStruct((rows, lanes), dtype) for rows in shapes],
        compiler_params=pltpu.CompilerParams(vmem_limit_bytes=60 * 2**20),
    )(jnp.stack(places), *values)


def join_body(mine_ref, *refs, count, stacked):
    row = 0
    for i in range(count):
        share, arrived = refs[2 * i], refs[2 * i + 1]
        out = refs[2 * count + (0 if stacked else i)]
        rows = share.shape[0]
        mine = mine_ref[i]
        out[pl.ds(pl.multiple_of(row + mine * rows, 16), rows), :] = share[...]
        out[pl.ds(pl.multiple_of(row + (1 - mine) * rows, 16), rows), :] = arrived[...]
        if stacked:
            row += 2 * rows


def join_parts(parts, stacked=False):
    if any(share.shape[0] % 16 for share, _, _ in parts):
        joined = [
            jnp.concatenate([jnp.where(mine == 1, b, a), jnp.where(mine == 1, a, b)], axis=0)
            for a, b, mine in parts
        ]
        return [jnp.concatenate(joined, axis=0)] if stacked else joined
    outs = [2 * a.shape[0] for a, _, _ in parts]
    if stacked:
        outs = [sum(outs)]
    lanes = parts[0][0].shape[1]
    whole = lambda rows: pl.BlockSpec((rows, lanes), lambda j, *_: (0, 0))
    return pl.pallas_call(
        functools.partial(join_body, count=len(parts), stacked=stacked),
        grid_spec=pltpu.PrefetchScalarGridSpec(
            num_scalar_prefetch=1,
            grid=(1,),
            in_specs=[whole(v.shape[0]) for a, b, _ in parts for v in (a, b)],
            out_specs=[whole(rows) for rows in outs],
        ),
        out_shape=[jax.ShapeDtypeStruct((rows, lanes), BF16) for rows in outs],
        compiler_params=pltpu.CompilerParams(vmem_limit_bytes=60 * 2**20),
    )(jnp.stack([mine for _, _, mine in parts]), *[v for a, b, _ in parts for v in (a, b)])


class Group:
    def __init__(self, pieces, rows, routes):
        self.parts = [
            {"pieces": [(piece, at) for piece in pieces], "rows": count, "route": route}
            for at, count, route in zip(
                [sum(rows[:i]) for i in range(len(rows))], rows, routes
            )
        ]
        self.levels = len(routes[0])
        self.level = 0
        self.flying = None
        self.shares = None

    def work(self, arrays, flying):
        level = self.level
        if level > self.levels:
            back = 2 * self.levels - level
            return join_parts(
                [
                    (share, arrived, upper(part["route"][back]))
                    for share, arrived, part in zip(self.shares, flying, self.parts)
                ],
                stacked=level == 2 * self.levels,
            )
        wanted = []
        for i, part in enumerate(self.parts):
            pieces = list(zip(arrays[i], [at for _, at in part["pieces"]]))
            if level:
                mine = upper(part["route"][level - 1])
                pieces = [(a, at + mine * part["rows"]) for a, at in pieces]
                pieces.append((flying[i], 0))
            part["pieces"] = pieces
            if level < self.levels:
                part["rows"] //= 2
                away = 1 - upper(part["route"][level])
                pieces = [(a, at + away * part["rows"]) for a, at in pieces]
            wanted.append((part["rows"], pieces))
        return sum_parts(wanted, F32 if level < self.levels else BF16)

    def step(self, held=()):
        arrays = [[a for a, _ in part["pieces"]] for part in self.parts]
        values = self.work(arrays, self.flying)
        values, held = tie(values, held)
        if self.level >= self.levels:
            self.shares = values
        if self.level < 2 * self.levels:
            next_level = min(self.level, 2 * self.levels - 1 - self.level)
            self.flying = [
                swap(value, part["route"][next_level]) for value, part in zip(values, self.parts)
            ]
        self.level += 1
        return held

    def done(self):
        return self.level > 2 * self.levels


def tie(*values):
    return lax.optimization_barrier(values)


def gelu_pair(values):
    logistic = jax.nn.sigmoid(1.702 * values)
    return (values * logistic, logistic + 1.702 * values * logistic * (1.0 - logistic))


def rows_product(former, latter):
    return lax.dot_general(
        former, latter, (((0,), (0,)), ((), ())), preferred_element_type=F32
    )


def back_product(former, latter):
    return lax.dot_general(
        former, latter, (((1,), (1,)), ((), ())), preferred_element_type=F32
    )


def taps(padded_rows, span):
    windows = padded_rows.shape[0]
    return [
        padded_rows[:, k * DILATION_STEP : k * DILATION_STEP + span, :].reshape(
            windows * span, -1
        )
        for k in range(3)
    ]


def statistics(plain_sum, square_sum, population):
    centre = plain_sum / population
    return (centre, lax.rsqrt(square_sum / population - centre * centre + EPS))


def edges(shard, width):
    peers, length = (lax.axis_size(BINS), shard.shape[1])
    up = [(i, i + 1) for i in range(peers - 1)]
    down = [(i + 1, i) for i in range(peers - 1)]
    return (
        (shard[:, length - width :], lambda value: lax.ppermute(value, BINS, up)),
        (shard[:, :width], lambda value: lax.ppermute(value, BINS, down)),
    )


def poisson_slope(logits, counted):
    held = jnp.maximum(logits, -80.0)
    small = jnp.exp(-jnp.abs(held))
    whole = 1.0 + small
    tail = jnp.where(small < 1e-3, small * (1.0 - 0.5 * small), jnp.log(whole))
    rate = jnp.maximum(held, 0.0) + tail
    top = jnp.where(held >= 0.0, 1.0, small)
    return top * (rate - counted) / (whole * rate)


def head_body(
    species_ref,
    windows_ref,
    humans_ref,
    mouse_ref,
    human_ref,
    bias_mouse_ref,
    bias_human_ref,
    counts_ref,
    rows_ref,
    columns_ref,
    out_ref,
    grads_ref,
    bias_grad_ref,
    weight_ref,
    bias_ref,
    sums_ref,
    *,
    mouse_tiles,
    tracks,
    scales,
):
    step = pl.program_id(0)
    tile, width = weight_ref.shape
    windows = windows_ref.shape[0]
    span = rows_ref.shape[0] // windows
    lane = counts_ref.shape[1]
    groups = span // lane
    is_mouse = step < mouse_tiles
    humans = humans_ref[0]
    active = jnp.where(is_mouse, windows - humans, humans)
    skipped = jnp.where(is_mouse, humans, 0)
    first = jnp.where(is_mouse, step, step - mouse_tiles) * tile
    end = jnp.where(is_mouse, tracks[1], tracks[0])
    scale = jnp.where(is_mouse, scales[1], scales[0]).astype(F32)

    def prepare():
        inside = first + lax.broadcasted_iota(jnp.int32, (tile, 1), 0) < end

        @pl.when(is_mouse)
        def _():
            weight_ref[...] = jnp.where(inside, mouse_ref[...], BF16(0))
            bias_ref[...] = jnp.broadcast_to(bias_mouse_ref[...], (LANES, tile)).T

        @pl.when(jnp.logical_not(is_mouse))
        def _():
            weight_ref[...] = jnp.where(inside, human_ref[...], BF16(0))
            bias_ref[...] = jnp.broadcast_to(bias_human_ref[...], (LANES, tile)).T

    def slopes(logits, window, scale):
        inside = first + lax.broadcasted_iota(jnp.int32, (tile, 1), 0) < end
        total = jnp.zeros((tile, lane), F32)
        low = []
        for h in range(groups):
            counted = counts_ref[
                pl.ds(h * windows + window, tile, stride=groups * windows), :
            ].astype(F32)
            part = logits[:, h * lane : (h + 1) * lane] + bias_ref[:, :lane]
            slope = jnp.where(inside, poisson_slope(part, counted) * scale, 0.0)
            total = total + slope
            low.append(slope.astype(BF16))
        return total, jnp.concatenate(low, axis=1)

    @pl.when(active == 0)
    def _():
        out_ref[...] = jnp.zeros_like(out_ref)
        grads_ref[...] = jnp.zeros_like(grads_ref)
        bias_grad_ref[...] = jnp.zeros_like(bias_grad_ref)

    @pl.when(active * 4 >= windows * 3)
    def _():
        prepare()
        total = None
        for i in range(windows):
            lanes = slice(i * span, (i + 1) * span)
            logits = jnp.dot(weight_ref[...], columns_ref[:, lanes], preferred_element_type=F32)
            part, low = slopes(
                logits, i, jnp.where((species_ref[i] == 1) == is_mouse, scale, 0.0)
            )
            total = part if total is None else total + part
            grads_ref[:, lanes] = low
        bias_grad_ref[...] = jnp.sum(total.T, axis=0, keepdims=True)
        product = jnp.dot(grads_ref[...], rows_ref[...], preferred_element_type=F32)
        out_ref[...] = product.astype(BF16)

    @pl.when((active > 0) & (active * 4 < windows * 3))
    def _():
        prepare()
        grads_ref[...] = jnp.zeros_like(grads_ref)
        sums_ref[...] = jnp.zeros_like(sums_ref)

        def one(window):
            at = window * span
            lanes = pl.ds(at if isinstance(window, int) else pl.multiple_of(at, span), span)
            logits = jnp.dot(weight_ref[...], columns_ref[:, lanes], preferred_element_type=F32)
            part, low = slopes(logits, window, scale)
            sums_ref[...] += part
            grads_ref[:, lanes] = low
            return 0

        if span % LANES == 0:
            lax.fori_loop(0, active, lambda i, _: one(windows_ref[skipped + i]), 0)
        else:
            for i in range(windows):

                @pl.when((species_ref[i] == 1) == is_mouse)
                def _():
                    one(i)
        bias_grad_ref[...] = jnp.sum(sums_ref[...].T, axis=0, keepdims=True)
        product = jnp.dot(grads_ref[...], rows_ref[...], preferred_element_type=F32)
        out_ref[...] = product.astype(BF16)


def head(
    species, order, humans, mouse, human, bias_mouse, bias_human, counts, rows, columns, scales
):
    tokens, width = rows.shape
    lane = counts.shape[1]
    tracks = (human.shape[0], mouse.shape[0])
    mouse_tiles = pl.cdiv(tracks[1], TILE)
    tiles = mouse_tiles + pl.cdiv(tracks[0], TILE)
    at_mouse = lambda j: jnp.minimum(j, mouse_tiles - 1)
    at_human = lambda j: jnp.maximum(j - mouse_tiles, 0)
    at_both = lambda j: jnp.where(j < mouse_tiles, j, j - mouse_tiles)
    fixed = lambda j, *_: (0, 0)
    out = lambda j, *_: (j, 0)
    return pl.pallas_call(
        functools.partial(head_body, mouse_tiles=mouse_tiles, tracks=tracks, scales=scales),
        grid_spec=pltpu.PrefetchScalarGridSpec(
            num_scalar_prefetch=3,
            grid=(tiles,),
            in_specs=[
                pl.BlockSpec((TILE, width), lambda j, *_: (at_mouse(j), 0)),
                pl.BlockSpec((TILE, width), lambda j, *_: (at_human(j), 0)),
                pl.BlockSpec((1, TILE), lambda j, *_: (0, at_mouse(j))),
                pl.BlockSpec((1, TILE), lambda j, *_: (0, at_human(j))),
                pl.BlockSpec((TILE * tokens // lane, lane), lambda j, *_: (at_both(j), 0)),
                pl.BlockSpec((tokens, width), fixed),
                pl.BlockSpec((width, tokens), fixed),
            ],
            out_specs=[
                pl.BlockSpec((TILE, width), out),
                pl.BlockSpec((TILE, tokens), out),
                pl.BlockSpec((1, TILE), lambda j, *_: (0, j)),
            ],
            scratch_shapes=[
                pltpu.VMEM((TILE, width), BF16),
                pltpu.VMEM((TILE, LANES), F32),
                pltpu.VMEM((TILE, lane), F32),
            ],
        ),
        out_shape=[
            jax.ShapeDtypeStruct((tiles * TILE, width), BF16),
            jax.ShapeDtypeStruct((tiles * TILE, tokens), BF16),
            jax.ShapeDtypeStruct((1, tiles * TILE), F32),
        ],
        compiler_params=pltpu.CompilerParams(vmem_limit_bytes=58 * 2**20),
        cost_estimate=pl.CostEstimate(
            flops=4 * tiles * TILE * width * tokens,
            bytes_accessed=tiles * TILE * (tokens * 6 + width * 4),
            transcendentals=3 * tiles * TILE * tokens,
        ),
    )(species, order, humans, mouse, human, bias_mouse, bias_human, counts, rows, columns)


def back_body(
    humans_ref, mouse_ref, human_ref, grads_ref, out_ref, total_ref, *, mouse_tiles, tracks, windows
):
    step = pl.program_id(0)
    tile = mouse_ref.shape[0]
    is_mouse = step < mouse_tiles
    row = lax.broadcasted_iota(jnp.int32, (tile, 1), 0)

    @pl.when(step == 0)
    def _():
        total_ref[...] = jnp.zeros_like(total_ref)

    @pl.when(is_mouse & (humans_ref[0] < windows))
    def _():
        inside = step * tile + row < tracks[1]
        weight = jnp.where(inside, mouse_ref[...], BF16(0)).T
        total_ref[...] += jnp.dot(weight, grads_ref[...], preferred_element_type=F32)

    @pl.when((step >= mouse_tiles) & (humans_ref[0] > 0))
    def _():
        inside = (step - mouse_tiles) * tile + row < tracks[0]
        weight = jnp.where(inside, human_ref[...], BF16(0)).T
        total_ref[...] += jnp.dot(weight, grads_ref[...], preferred_element_type=F32)

    @pl.when(step == pl.num_programs(0) - 1)
    def _():
        out_ref[...] = total_ref[...].T


def head_back(humans, windows, mouse, human, grads):
    tokens = grads.shape[1]
    width = human.shape[1]
    mouse_tiles = pl.cdiv(mouse.shape[0], TILE)
    tiles = grads.shape[0] // TILE
    return pl.pallas_call(
        functools.partial(
            back_body,
            mouse_tiles=mouse_tiles,
            tracks=(human.shape[0], mouse.shape[0]),
            windows=windows,
        ),
        grid_spec=pltpu.PrefetchScalarGridSpec(
            num_scalar_prefetch=1,
            grid=(tiles,),
            in_specs=[
                pl.BlockSpec((TILE, width), lambda j, *_: (jnp.minimum(j, mouse_tiles - 1), 0)),
                pl.BlockSpec((TILE, width), lambda j, *_: (jnp.maximum(j - mouse_tiles, 0), 0)),
                pl.BlockSpec((TILE, tokens), lambda j, *_: (j, 0)),
            ],
            out_specs=pl.BlockSpec((tokens, width), lambda j, *_: (0, 0)),
            scratch_shapes=[pltpu.VMEM((width, tokens), F32)],
        ),
        out_shape=jax.ShapeDtypeStruct((tokens, width), F32),
        compiler_params=pltpu.CompilerParams(vmem_limit_bytes=58 * 2**20),
        cost_estimate=pl.CostEstimate(
            flops=2 * tiles * TILE * width * tokens,
            bytes_accessed=tiles * TILE * (tokens + width) * 2,
            transcendentals=0,
        ),
    )(humans, mouse, human, grads)


def widen_body(in_ref, out_ref):
    out_ref[...] = in_ref[0].astype(F32)


def widen_head(tracks, summed, first):
    _, block, width = summed.shape
    return pl.pallas_call(
        widen_body,
        grid=(pl.cdiv(tracks, block),),
        in_specs=[pl.BlockSpec((1, block, width), lambda j: (first // block + j, 0, 0))],
        out_specs=pl.BlockSpec((block, width), lambda j: (j, 0)),
        out_shape=jax.ShapeDtypeStruct((tracks, width), F32),
        compiler_params=pltpu.CompilerParams(vmem_limit_bytes=60 * 2**20),
    )(summed)


def weights_body(core_ref, mine_ref, other_ref, conv_ref, proj_ref, sums_ref):
    half, middle = mine_ref.shape
    taken = conv_ref.shape[0]
    strips = proj_ref.shape[1] // middle

    def spread(first, second):
        def rows(start, count):
            parts = []
            if start < half:
                parts.append(first[start : min(half, start + count), :])
            if start + count > half:
                parts.append(second[max(0, start - half) : start + count - half, :])
            parts = [part.astype(F32) for part in parts]
            return parts[0] if len(parts) == 1 else jnp.concatenate(parts, axis=0)

        conv_ref[...] = rows(0, taken)
        for i in range(strips):
            proj_ref[:, i * middle : (i + 1) * middle] = rows(
                taken + i * proj_ref.shape[0], proj_ref.shape[0]
            )
        sums_ref[...] = rows(taken + strips * proj_ref.shape[0], sums_ref.shape[0])

    @pl.when(core_ref[0] == 0)
    def _():
        spread(mine_ref, other_ref)

    @pl.when(core_ref[0] != 0)
    def _():
        spread(other_ref, mine_ref)


def finish_weights(core, mine, other, taken, proj_shape):
    half, middle = mine.shape
    rest = 2 * half - taken - proj_shape[0] * proj_shape[1] // middle
    shapes = [(taken, middle), proj_shape, (rest, middle)]
    whole = lambda shape: pl.BlockSpec(shape, lambda j, *_: (0, 0))
    return pl.pallas_call(
        weights_body,
        grid_spec=pltpu.PrefetchScalarGridSpec(
            num_scalar_prefetch=1,
            grid=(1,),
            in_specs=[whole((half, middle))] * 2,
            out_specs=[whole(shape) for shape in shapes],
        ),
        out_shape=[jax.ShapeDtypeStruct(shape, F32) for shape in shapes],
        compiler_params=pltpu.CompilerParams(vmem_limit_bytes=60 * 2**20),
    )(core, mine, other)


def on_device(
    block_in,
    gain_in,
    shift_in,
    dilated_taps_weight,
    gain_mid,
    shift_mid,
    proj_weight,
    proj_bias,
    head_human,
    bias_human,
    head_mouse,
    bias_mouse,
    species,
    counts,
):
    windows, span, width = block_in.shape
    tokens = windows * span
    middle = proj_weight.shape[0]
    tracks_human = head_human.shape[1]
    tracks_mouse = head_mouse.shape[1]
    devices = lax.axis_size(EVERY)
    population = float(tokens * devices)
    core = lax.axis_index("core").astype(jnp.int32)[None]

    wide = block_in.reshape(tokens, width).astype(F32)
    sent, finish = small_sum([jnp.sum(wide, axis=0), jnp.sum(wide * wide, axis=0)])
    before, after = [move(value) for value, move in edges(block_in, DILATION_STEP)]
    everyone = to_all(sent)
    sum_in, square_in = finish(everyone)
    centre_in, scale_in = statistics(sum_in, square_in, population)

    def activate_in(values):
        return gelu_pair((values.astype(F32) - centre_in) * scale_in * gain_in + shift_in)

    normed_in = (wide - centre_in) * scale_in
    hidden_in, slope_in = gelu_pair(normed_in * gain_in + shift_in)
    hidden_in = hidden_in.astype(BF16).reshape(windows, span, width)
    place = lax.axis_index(BINS)
    last = lax.axis_size(BINS) - 1
    hidden_before = jnp.where(place > 0, activate_in(before)[0], 0.0).astype(BF16)
    hidden_after = jnp.where(place < last, activate_in(after)[0], 0.0).astype(BF16)
    padded = jnp.concatenate([hidden_before, hidden_in, hidden_after], axis=1)
    shifted = taps(padded, span)
    dilated = sum(
        jnp.dot(rows, dilated_taps_weight[k], preferred_element_type=F32)
        for k, rows in enumerate(shifted)
    )
    sent, finish = small_sum([jnp.sum(dilated, axis=0), jnp.sum(dilated * dilated, axis=0)])
    sum_mid, square_mid = finish(to_all(sent))
    centre_mid, scale_mid = statistics(sum_mid, square_mid, population)
    normed_mid = (dilated - centre_mid) * scale_mid
    hidden_mid, slope_mid = gelu_pair(normed_mid * gain_mid + shift_mid)
    hidden_mid = hidden_mid.astype(BF16)
    branch = jnp.dot(hidden_mid, proj_weight, preferred_element_type=F32)
    block_out = (wide + branch + proj_bias).astype(BF16)

    lane = min(span, LANES)
    counts_rows = (
        counts.transpose(2, 0, 1)
        .reshape(tracks_human, windows, span // lane, lane)
        .transpose(0, 2, 1, 3)
        .reshape(-1, lane)
    )
    columns = block_out.T
    scales = (math.sqrt(width / tracks_human), math.sqrt(width / tracks_mouse))
    by_species = jnp.argsort(species).astype(jnp.int32)
    humans = jnp.sum(species == 0).astype(jnp.int32)[None]
    mouse_tiles, human_tiles = pl.cdiv(tracks_mouse, TILE), pl.cdiv(tracks_human, TILE)
    mouse, human = head_mouse.T, head_human.T

    scatter = lambda value, axes: lax.psum_scatter(value, axes, scatter_dimension=0, tiled=True)
    gather = lambda value, axes: lax.all_gather(value, axes)
    across, along, deep = bits_of("x"), bits_of("y"), bits_of("batch")
    grads, slopes, bias_grads = head(
        species, by_species, humans, mouse, human, bias_mouse[None], bias_human[None],
        counts_rows, block_out, columns, scales,
    )
    summed = scatter(grads, BINS)
    output_grad = head_back(humans, windows, mouse, human, slopes)
    to_core = lambda value: swap(value, CORE)
    chips = lax.axis_size(CHIPS)

    def after_head(output_grad):
        branch_grad = output_grad.astype(BF16)
        mid_grad = back_product(branch_grad, proj_weight) * slope_mid
        sent, _ = small_sum([jnp.sum(mid_grad, axis=0), jnp.sum(mid_grad * normed_mid, axis=0)])
        return sent, branch_grad, mid_grad

    sent, branch_grad, mid_grad = after_head(output_grad)
    everyone = to_all(sent)

    def weight_work(branch_grad, output_grad):
        product = rows_product(hidden_mid, branch_grad).reshape(middle, width // middle, middle)
        return product.swapaxes(0, 1).reshape(-1, middle), jnp.sum(output_grad, axis=0)

    proj_grad, proj_bias_grad = weight_work(branch_grad, output_grad)

    def middle_work(everyone, mid_grad):
        _, finish = small_sum([shift_mid, gain_mid])
        shift_mid_grad, gain_mid_grad = finish(everyone)
        dilated_grad = scale_mid * gain_mid * (
            mid_grad - shift_mid_grad / population - normed_mid * gain_mid_grad / population
        )
        return dilated_grad.astype(BF16), shift_mid_grad, gain_mid_grad

    dilated_grad, shift_mid_grad, gain_mid_grad = middle_work(everyone, mid_grad)
    dilated_windows = dilated_grad.reshape(windows, span, middle)
    grad_before, grad_after = [move(value) for value, move in edges(dilated_windows, DILATION_STEP)]
    sums = jnp.concatenate(
        [
            proj_bias_grad,
            bias_grads[0, mouse_tiles * TILE : mouse_tiles * TILE + tracks_human],
            bias_grads[0, :tracks_mouse],
        ]
    )
    vector_rows = pl.cdiv(sums.size, middle)
    grain = 32 * chips
    all_rows = pl.cdiv(4 * width + vector_rows, grain) * grain
    half = all_rows // 2

    def conv_work(dilated_grad, proj_grad, sums):
        parts = [rows_product(rows, dilated_grad) for rows in shifted] + [proj_grad]
        rows = jnp.pad(sums, (0, vector_rows * middle - sums.size)).reshape(-1, middle)
        parts.append(jnp.pad(rows, ((0, all_rows - 4 * width - vector_rows), (0, 0))))
        grads = jnp.concatenate(parts, axis=0)
        return lax.dynamic_slice_in_dim(grads, (1 - core[0]) * half, half, 0), grads

    weights_send, weights_grad = conv_work(dilated_grad, proj_grad, sums)
    weights_arrived = to_core(weights_send)
    weights_keep = lax.dynamic_slice_in_dim(weights_grad, core[0] * half, half, 0)
    weights = Group(
        [weights_keep, weights_arrived],
        [half // 2] * 2,
        (across + along + deep, along + across + deep),
    )
    grad_before = weights.step(grad_before)

    def hidden_work(grad_before, dilated_windows, grad_after):
        grad_shifted = taps(
            jnp.concatenate([grad_before, dilated_windows, grad_after], axis=1), span
        )
        hidden_grad = sum(
            back_product(grad_shifted[2 - k], dilated_taps_weight[k]) for k in range(3)
        )
        in_grad = hidden_grad * slope_in
        sent, _ = small_sum([jnp.sum(in_grad, axis=0), jnp.sum(in_grad * normed_in, axis=0)])
        return sent, in_grad

    sent, in_grad = hidden_work(grad_before, dilated_windows, grad_after)
    everyone = to_all(sent)
    summed, in_grad = tie(summed, in_grad)
    summed = scatter(summed, "batch")
    summed = weights.step(summed)
    summed = gather(summed, "batch").reshape(-1, width)
    everyone = weights.step(everyone)
    summed = weights.step(summed)
    summed = gather(summed, BINS)

    def last_work(everyone, output_grad, in_grad):
        _, finish = small_sum([shift_in, gain_in])
        shift_in_grad, gain_in_grad = finish(everyone)
        input_grad = output_grad + scale_in * gain_in * (
            in_grad - shift_in_grad / population - normed_in * gain_in_grad / population
        )
        return input_grad.astype(BF16), shift_in_grad, gain_in_grad

    input_grad, shift_in_grad, gain_in_grad = last_work(everyone, output_grad, in_grad)
    while weights.level < 2 * weights.levels - 1:
        weights.step()
    input_grad = weights.step(input_grad)
    while not weights.done():
        weights.step()
    weights_mine = weights.shares[0]
    weights_other = to_core(weights_mine)
    summed = summed.reshape(lax.axis_size(BINS), -1, width)
    head_mouse_grad = widen_head(tracks_mouse, summed, 0)
    head_human_grad = widen_head(tracks_human, summed, mouse_tiles * TILE)
    weights_other, head_mouse_grad, head_human_grad = tie(
        weights_other, head_mouse_grad, head_human_grad
    )
    conv_total, proj_total, sums_total = finish_weights(
        core, weights_mine, weights_other, 3 * width, (middle, width)
    )
    conv_total = conv_total.reshape(3, width, middle)
    sums_total = sums_total[:vector_rows].reshape(-1)
    ends = [0, width, width + tracks_human, width + tracks_human + tracks_mouse]
    proj_bias_total, bias_human_grad, bias_mouse_grad = [
        sums_total[low:high] for low, high in zip(ends[:-1], ends[1:])
    ]
    return (
        block_out.reshape(windows, span, width),
        input_grad.reshape(windows, span, width),
        gain_in_grad,
        shift_in_grad,
        conv_total,
        gain_mid_grad,
        shift_mid_grad,
        proj_total,
        proj_bias_total,
        head_human_grad.T,
        bias_human_grad,
        head_mouse_grad.T,
        bias_mouse_grad,
    )


def solution(mesh):
    bins, batch = mesh.shape["bins"], mesh.shape["batch"]
    side = 1 << (((bins // 2).bit_length() - 1) // 2)
    grid = jax.sharding.Mesh(
        mesh.devices.reshape(bins // 2 // side, side, 2, batch), ("y", "x", "core", "batch")
    )
    tokens = P("batch", BINS, None)
    placed = (tokens,) + (P(),) * 11 + (P("batch"), tokens)
    return jax.shard_map(
        on_device,
        mesh=grid,
        in_specs=placed,
        out_specs=(tokens, tokens) + (P(),) * 11,
        check_vma=False,
    )
```
